512 devices in a mesh: ctx: 32 (over x_lo, z, core), heads: 16 (over x_hi, y).
Axes of the slice: x: 4 (x_hi: 2, x_lo: 2; x = x_hi * 2 + x_lo), y: 8, z: 8, core: 2. Of those that a mesh axis runs over, the one named last changes fastest.
Arguments:
- queries: bfloat16 [8192, 8192], P('ctx', 'heads'), may hold values from -6 to 6
- keys: bfloat16 [8192, 8192], P('ctx', 'heads'), may hold values from -6 to 6
- values: bfloat16 [8192, 8192], P('ctx', 'heads'), may hold values from -60 to 60
- hyena_inputs: bfloat16 [3, 8192, 8192], P(None, 'ctx', 'heads'), may hold values from -6 to 6
- hyena_filter: float32 [7, 8192], P(None, 'heads'), may hold values from -2.4 to 2.4
- norm_gain: float32 [8192], P('heads'), may hold values from 0.5 to 1.5
Outputs:
- mixed: bfloat16 [8192, 8192], P('ctx', 'heads')
The draws below stay inside these ranges and needn't reach their ends.
All inputs are finite; a program needn't handle non-finite values.
Results may differ from the reference program's by a relative error of at most 0.009.
Values may be sent and summed in bfloat16 or wider, within the bound.
No kernel may reach another device: no remote copies, remote signals or barrier semaphores. Data moves between devices by JAX's collectives and lax.ppermute only.
A program may use at most 64 MiB of HBM per device.

```python
import math
import jax
import jax.numpy as jnp
from jax import lax

HEADS = 64
DH = 128
FILT = 7
WIDTH = 8192
SEQ = 8192


def base_draw(key):
    return jnp.clip(jax.random.normal(key, (SEQ, WIDTH), jnp.float32), -5.0, 5.0)


def draw_queries(key, part):
    result = base_draw(jax.random.fold_in(key, 1))
    return result.astype(jnp.bfloat16)


def draw_keys(key, part):
    result = base_draw(jax.random.fold_in(key, 2))
    return result.astype(jnp.bfloat16)


def draw_values(key, part):
    result = base_draw(jax.random.fold_in(key, 3))
    column_place = jnp.arange(WIDTH, dtype=jnp.float32)[None, :] / WIDTH
    row_level = jax.random.uniform(jax.random.fold_in(key, 4), (SEQ, 1), jnp.float32, 0.0, 1.0)
    column_scale = jnp.power(10.0, column_place - 0.5)
    row_scale = jnp.power(10.0, row_level - 0.5)
    return (result * column_scale * row_scale).astype(jnp.bfloat16)


def block_scale(stream_key, extent, pieces, least, largest):
    gain = 1.0
    for axis_at, parts in pieces:
        heights = jax.random.uniform(jax.random.fold_in(jax.random.fold_in(stream_key, 6), axis_at), (parts,), jnp.float32, least / len(pieces), largest / len(pieces))
        gain = gain * jnp.repeat(jnp.exp(heights), extent[axis_at] // parts).reshape((-1,) + (1,) * (len(extent) - 1 - axis_at))
    return gain


def normal_values(stream_key, shape, scale, limit, split=(), kind=jnp.bfloat16):
    values = jax.random.normal(stream_key, shape, jnp.float32) * scale
    if len(split) > 0:
        values = block_scale(stream_key, shape, split, -0.22, 0.18) * values
    return jnp.clip(values, min=-limit, max=limit).astype(kind)


def setup_inputs(seed: int = 0) -> dict:
    key_list = jax.random.split(jax.random.key(seed), 7)
    return {
        "queries": draw_queries(jax.random.fold_in(key_list[6], 71), 0),
        "keys": draw_keys(jax.random.fold_in(key_list[6], 71), 0),
        "values": draw_values(jax.random.fold_in(key_list[6], 71), 0),
        "hyena_inputs": normal_values(key_list[3], (3, SEQ, WIDTH), 1.0, 6.0, ((1, 32), (2, 16))),
        "hyena_filter": normal_values(key_list[4], (FILT, WIDTH), 0.4, 2.4, ((1, 16),), jnp.float32),
        "norm_gain": jnp.clip(1.0 + 0.1 * jax.random.normal(key_list[5], (WIDTH,), jnp.float32), 0.5, 1.5),
    }


def head_attention(query_head, key_head, value_head):
    block_rows = math.gcd(SEQ, 1024)
    key_place = jnp.arange(SEQ, dtype=jnp.int32)
    score_scale = 1.0 / math.sqrt(DH)

    def one_block(block_start):
        query_block = lax.dynamic_slice_in_dim(query_head, block_start, block_rows, 0)
        scores = jnp.dot(query_block, key_head.T, preferred_element_type=jnp.float32) * score_scale
        query_place = block_start + jnp.arange(block_rows, dtype=jnp.int32)
        visible = key_place[None, :] <= query_place[:, None]
        scores = jnp.where(visible, scores, -1e+30)
        row_top = lax.optimization_barrier(jnp.max(scores, axis=1, keepdims=True))
        weights = jnp.where(visible, jnp.exp(scores - row_top), 0.0)
        totals = lax.optimization_barrier(jnp.sum(weights, axis=1, keepdims=True))
        summed = jnp.dot(weights.astype(jnp.bfloat16), value_head, preferred_element_type=jnp.float32)
        return summed / totals
    starts = (jnp.arange(SEQ // block_rows, dtype=jnp.int32) * block_rows).astype(jnp.int32)
    return lax.map(one_block, starts).reshape(SEQ, DH)

def reference(queries, keys, values, hyena_inputs, hyena_filter, norm_gain):

    def split_heads(array):
        return jnp.transpose(array.reshape(SEQ, HEADS, DH), (1, 0, 2))
    per_head = lax.map(lambda triple: head_attention(triple[0], triple[1], triple[2]), (split_heads(queries), split_heads(keys), split_heads(values)))
    attention = jnp.transpose(per_head, (1, 0, 2)).reshape(SEQ, WIDTH).astype(jnp.bfloat16)
    attention_wide = lax.optimization_barrier(attention).astype(jnp.float32)
    square_mean = lax.optimization_barrier(jnp.sum(attention_wide * attention_wide, axis=1)) / WIDTH
    product = hyena_inputs[1].astype(jnp.float32) * hyena_inputs[2].astype(jnp.float32)
    padded = jnp.concatenate([jnp.zeros((FILT - 1, WIDTH), jnp.float32), product], axis=0)
    convolved = jnp.zeros((SEQ, WIDTH), jnp.float32)
    for filter_tap in range(FILT):
        convolved = convolved + hyena_filter[filter_tap][None, :] * padded[FILT - 1 - filter_tap:FILT - 1 - filter_tap + SEQ]
    hyena_out = hyena_inputs[0].astype(jnp.float32) * convolved
    normed = attention_wide * lax.rsqrt(square_mean + 1e-06)[:, None] * norm_gain[None, :]
    return (normed + hyena_out).astype(jnp.bfloat16)
```

```python
import functools
import math

import jax
import jax.numpy as jnp
from jax import lax
from jax.experimental import pallas as pl
from jax.experimental.pallas import tpu as pltpu
from jax.sharding import PartitionSpec as P

DH = 128
WIDTH = 8192
Z = 8
ROWS = 256
SCALE2 = math.log2(math.e) / math.sqrt(DH)
LOW = -1e29
HIDDEN = -1e30
F32 = jnp.float32
BF16 = jnp.bfloat16


def chip(x, z, c):
    return (x * Z + z % Z) * 2 + c


RING = [
    (chip(x, z, c), chip(x, z + 1 - 2 * c, c)) for x in range(2) for z in range(Z) for c in range(2)
]
CORES = [(chip(x, z, c), chip(x, z, 1 - c)) for x in range(2) for z in range(Z) for c in range(2)]
DOWN = [(chip(1, z, c), chip(0, z, c)) for z in range(Z) for c in range(2)]
UP = [(chip(0, z, c), chip(1, z, c)) for z in range(Z) for c in range(2)]


def lanes(shape):
    return lax.broadcasted_iota(jnp.int32, shape, 1)


def place_columns(columns):
    lane = lanes((ROWS, 128))
    result = jnp.zeros((ROWS, 128), F32)
    for number, column in columns:
        result = jnp.where(lane == number, column, result)
    return result


def exact_parts(value):
    high = value.astype(BF16).astype(F32)
    rest = value - high
    middle = rest.astype(BF16).astype(F32)
    return high, middle, rest - middle


def attend_kernel(chunk_count, first, last, heads, where_ref, q_ref, *refs):
    chunks = refs[:chunk_count]
    refs = refs[chunk_count:]
    if not first:
        acc_in, stat_in = refs[:2]
        refs = refs[2:]
    tile = pl.program_id(0)
    above = where_ref[0]

    def run(masked):
        if masked:
            query_start = where_ref[1 + tile]
            drift = lax.broadcasted_iota(jnp.int32, (ROWS, ROWS), 0) - lanes((ROWS, ROWS))
            seen = [drift >= where_ref[3 + j] - query_start for j in range(chunk_count)]
        columns = []
        for h in range(heads):
            span = slice(h * DH, (h + 1) * DH)
            query = q_ref[0, :, span]
            scores = []
            for j in range(chunk_count):
                score = lax.dot_general(
                    query, chunks[j][0, :, span], (((1,), (1,)), ((), ())), preferred_element_type=F32
                )
                if masked:
                    score = jnp.where(seen[j], score, HIDDEN)
                scores.append(score)
            top = jnp.max(functools.reduce(jnp.maximum, scores), axis=1, keepdims=True)
            if first:
                top = jnp.maximum(top, LOW)
            else:
                old_top = stat_in[0, :, h : h + 1]
                top = jnp.maximum(top, old_top)
                fade = jnp.exp2((old_top - top) * SCALE2)
            weights = [jnp.exp2((score - top) * SCALE2) for score in scores]
            total = jnp.sum(functools.reduce(jnp.add, weights), axis=1, keepdims=True)
            summed = None
            for j in range(chunk_count):
                part = jnp.dot(
                    weights[j].astype(BF16), chunks[j][1, :, span], preferred_element_type=F32
                )
                summed = part if summed is None else summed + part
            if not first:
                total = total + fade * stat_in[0, :, heads + h : heads + h + 1]
                summed = summed + fade * acc_in[0, :, span]
            if last:
                refs[0][0, :, span] = (summed / jnp.maximum(total, 1e-30)).astype(BF16)
                level = jnp.where(total > 0, top * SCALE2 + jnp.log2(jnp.maximum(total, 1e-30)), HIDDEN)
                for k, part in enumerate(exact_parts(level)):
                    columns.append((k * heads + h, part))
            else:
                refs[0][0, :, span] = summed
                columns.append((h, top))
                columns.append((heads + h, total))
        if last:
            refs[0][0, :, heads * DH :] = place_columns(columns).astype(BF16)
        else:
            refs[1][0] = place_columns(columns)

    @pl.when(tile < 2)
    def _():
        run(True)

    @pl.when((tile >= 2) & (above == 0))
    def _():
        run(False)

    if first or last:

        @pl.when((tile >= 2) & (above != 0))
        def _():
            for ref in refs:
                ref[...] = jnp.zeros(ref.shape, ref.dtype)


def attend_call(where, queries, chunks, state, last):
    first = state is None
    width = queries.shape[2]
    heads = width // DH
    tile = lambda cols: pl.BlockSpec((1, ROWS, cols), lambda i, *_: (i, 0, 0))
    whole = pl.BlockSpec((2, ROWS, width), lambda i, *_: (0, 0, 0))
    in_specs = [tile(width)] + [whole] * len(chunks)
    operands = [queries, *chunks]
    if not first:
        in_specs += [tile(width), tile(128)]
        operands += list(state)
    if last:
        out_shape = jax.ShapeDtypeStruct((4, ROWS, width + 128), BF16)
        out_specs = tile(width + 128)
        aliases = {}
    else:
        out_shape = (
            jax.ShapeDtypeStruct((4, ROWS, width), F32),
            jax.ShapeDtypeStruct((4, ROWS, 128), F32),
        )
        out_specs = (tile(width), tile(128))
        aliases = {} if first else {len(operands) - 1: 0, len(operands): 1}
    keys = ROWS * len(chunks)
    return pl.pallas_call(
        functools.partial(attend_kernel, len(chunks), first, last, heads),
        out_shape=out_shape,
        grid_spec=pltpu.PrefetchScalarGridSpec(
            num_scalar_prefetch=1, grid=(4,), in_specs=in_specs, out_specs=out_specs
        ),
        input_output_aliases=aliases,
        compiler_params=pltpu.CompilerParams(vmem_limit_bytes=32 * 1024 * 1024),
        cost_estimate=pl.CostEstimate(
            flops=4 * 4 * ROWS * keys * width,
            bytes_accessed=8 * ROWS * width * 4,
            transcendentals=4 * ROWS * keys * heads,
        ),
    )(where, *operands)


def level_of(ref_value, heads, h):
    wide = ref_value.astype(F32)
    return sum(wide[:, k * heads + h : k * heads + h + 1] for k in range(3))


def merged(parts, levels):
    top = functools.reduce(jnp.maximum, levels)
    shares = [jnp.exp2(level - top) for level in levels]
    total = functools.reduce(jnp.add, shares)
    blend = functools.reduce(
        jnp.add, [part.astype(F32) * share for part, share in zip(parts, shares)]
    )
    return blend / total, top + jnp.log2(total)


def merge_kernel(heads, a_ref, b_ref, o_ref):
    width = heads * DH
    tails = (a_ref[:, width:], b_ref[:, width:])
    columns = []
    for h in range(heads):
        span = slice(h * DH, (h + 1) * DH)
        out, level = merged(
            (a_ref[:, span], b_ref[:, span]), [level_of(tail, heads, h) for tail in tails]
        )
        o_ref[:, span] = out.astype(BF16)
        for k, part in enumerate(exact_parts(level)):
            columns.append((k * heads + h, part))
    o_ref[:, width:] = place_columns(columns).astype(BF16)


def merge_call(a, b):
    heads = a.shape[1] // DH - 1
    return pl.pallas_call(
        functools.partial(merge_kernel, heads), out_shape=jax.ShapeDtypeStruct(a.shape, BF16)
    )(a, b)


def combine_kernel(heads, where_ref, a_ref, b_ref, s_ref, att_ref, square_ref):
    width = heads * DH
    tails = [ref[:, width:] for ref in (a_ref, b_ref, s_ref)]
    squares = jnp.zeros((ROWS, DH), F32)
    for h in range(heads):
        span = slice(h * DH, (h + 1) * DH)
        levels = [level_of(tail, heads, h) for tail in tails]
        levels[2] = jnp.where(where_ref[0] != 0, levels[2], HIDDEN)
        out, _ = merged((a_ref[:, span], b_ref[:, span], s_ref[:, span]), levels)
        half = out.astype(BF16)
        att_ref[:, span] = half
        wide = half.astype(F32)
        squares = squares + wide * wide
    row_sums = jnp.sum(squares, axis=1, keepdims=True)
    square_ref[...] = jnp.broadcast_to(row_sums, (ROWS, 128)).T[: square_ref.shape[0]]


def combine_call(where, a, b, s, group):
    heads = a.shape[1] // DH - 1
    return pl.pallas_call(
        functools.partial(combine_kernel, heads),
        out_shape=(
            jax.ShapeDtypeStruct((ROWS, heads * DH), BF16),
            jax.ShapeDtypeStruct((group, ROWS), F32),
        ),
        in_specs=[pl.BlockSpec(memory_space=pltpu.SMEM)]
        + [pl.BlockSpec(memory_space=pltpu.VMEM)] * 3,
    )(where, a, b, s)


def hyena(hyena_inputs, hyena_filter):
    row_count, col_count = hyena_inputs.shape[1:]
    rim_rows = hyena_filter.shape[0] - 1
    size = lax.axis_size("ctx")
    earlier = lax.ppermute(
        hyena_inputs[1:, row_count - rim_rows :, :], "ctx", [(i, i + 1) for i in range(size - 1)]
    )
    joined = jnp.concatenate([earlier, hyena_inputs[1:]], axis=1)
    product = joined[0].astype(F32) * joined[1].astype(F32)
    convolved = jnp.zeros((row_count, col_count), F32)
    for tap in range(rim_rows + 1):
        start = rim_rows - tap
        convolved = convolved + hyena_filter[tap][None, :] * product[start : start + row_count]
    return hyena_inputs[0].astype(F32) * convolved


def on_device(queries, keys, values, hyena_inputs, hyena_filter, norm_gain):
    ctx = lax.axis_index("ctx")
    x, z, c = ctx // (2 * Z), (ctx // 2) % Z, ctx % 2
    toward = 2 * c - 1
    own = jnp.stack([keys, values])
    other = lax.ppermute(jnp.stack([keys, values, queries]), "ctx", CORES)
    a, b = [own], [other[:2]]
    for step in range(4):
        a.append(lax.ppermute(a[-1], "ctx", RING))
        if step < 3:
            b.append(lax.ppermute(b[-1], "ctx", RING))
    chip_queries = jnp.stack([queries, other[2]])
    queries_all = jnp.concatenate([chip_queries, lax.ppermute(chip_queries, "ctx", DOWN)])

    def where(*chunks):
        starts = [
            ((z + step * toward) % Z) * 2 * ROWS + (c if same else 1 - c) * ROWS
            for same, step in chunks
        ]
        rows = [z * 2 * ROWS + c * ROWS, z * 2 * ROWS + (1 - c) * ROWS]
        return jnp.stack([x, *rows, *starts]).astype(jnp.int32)

    state = attend_call(
        where((1, 0), (1, 1), (0, 1)), queries_all, [a[0], a[1], b[1]], None, False
    )
    state = attend_call(where((1, 2), (0, 2)), queries_all, [a[2], b[2]], state, False)
    state = attend_call(where((1, 3), (0, 3)), queries_all, [a[3], b[3]], state, False)
    parts = attend_call(where((1, 4)), queries_all, [a[4]], state, True)

    below = merge_call(parts[2], lax.ppermute(parts[3], "ctx", CORES))
    across = lax.ppermute(below, "ctx", UP)
    mine = lax.ppermute(parts[1], "ctx", CORES)
    group = lax.axis_size("heads")
    attention, squares = combine_call(
        x.astype(jnp.int32).reshape(1), parts[0], mine, across, group
    )
    spread = lax.all_to_all(squares, "heads", 0, 0, tiled=True)
    square_mean = jnp.sum(spread, axis=0) / WIDTH
    normed = attention.astype(F32) * lax.rsqrt(square_mean + 1e-06)[:, None] * norm_gain[None, :]
    return (normed + hyena(hyena_inputs, hyena_filter)).astype(BF16)


def solution(mesh):
    placed = (
        P("ctx", "heads"),
        P("ctx", "heads"),
        P("ctx", "heads"),
        P(None, "ctx", "heads"),
        P(None, "heads"),
        P("heads"),
    )
    return jax.shard_map(
        on_device, mesh=mesh, in_specs=placed, out_specs=P("ctx", "heads"), check_vma=False
    )
```

```python
import functools
import math

import jax
import jax.numpy as jnp
from jax import lax
from jax.experimental import pallas as pl
from jax.experimental.pallas import tpu as pltpu
from jax.sharding import PartitionSpec as P

DH = 128
WIDTH = 8192
Z = 8
ROWS = 256
SCALE2 = math.log2(math.e) / math.sqrt(DH)
LOW = -1e29
HIDDEN = -1e30
F32 = jnp.float32
BF16 = jnp.bfloat16


def chip(x, z, c):
    return (x * Z + z % Z) * 2 + c


RING = [
    (chip(x, z, c), chip(x, z + 1 - 2 * c, c)) for x in range(2) for z in range(Z) for c in range(2)
]
CORES = [(chip(x, z, c), chip(x, z, 1 - c)) for x in range(2) for z in range(Z) for c in range(2)]
DOWN = [(chip(1, z, c), chip(0, z, c)) for z in range(Z) for c in range(2)]
UP = [(chip(0, z, c), chip(1, z, c)) for z in range(Z) for c in range(2)]


def kept(shape, dtype):
    return pltpu.VMEM(shape, dtype)


def room(mebibytes):
    return pltpu.CompilerParams(vmem_limit_bytes=mebibytes * 1024 * 1024)


def rows_placed(count, numbered):
    row = lax.broadcasted_iota(jnp.int32, (count, ROWS), 0)
    result = jnp.zeros((count, ROWS), F32)
    for number, value in numbered:
        result = jnp.where(row == number, value, result)
    return result


def exact_parts(value):
    high = value.astype(BF16).astype(F32)
    rest = value - high
    middle = rest.astype(BF16).astype(F32)
    return high, middle, rest - middle


def prepare_kernel(heads, k_ref, v_ref, q_ref, pair_ref, triple_ref, held, sems):
    copies = [
        pltpu.make_async_copy(source, target, sems.at[number])
        for number, (source, target) in enumerate(
            (
                (v_ref, held),
                (k_ref, pair_ref.at[0]),
                (k_ref, triple_ref.at[0]),
                (q_ref, triple_ref.at[2]),
            )
        )
    ]
    for copy in copies:
        copy.start()
    copies[0].wait()
    for h in range(heads):
        turned = held[:, h * DH : (h + 1) * DH].T
        place = (slice(h % 2 * DH, (h % 2 + 1) * DH), slice(h // 2 * ROWS, (h // 2 + 1) * ROWS))
        for ref in (pair_ref, triple_ref):
            ref[(1, *place)] = turned
    for copy in copies[1:]:
        copy.wait()


def prepare_call(keys, values, queries):
    return pl.pallas_call(
        functools.partial(prepare_kernel, keys.shape[1] // DH),
        out_shape=tuple(kept((n, *keys.shape), BF16) for n in (2, 3)),
        in_specs=[pl.BlockSpec(memory_space=pl.ANY)] * 3,
        scratch_shapes=[pltpu.VMEM(values.shape, BF16), pltpu.SemaphoreType.DMA((4,))],
        compiler_params=room(56),
    )(keys, values, queries)


def attend_kernel(places, plan, last, heads, where_ref, *refs):
    query_refs = (refs[0].at[2], refs[1].at[2], refs[2], refs[3])
    held = refs[4 : 4 + len(places)]
    refs = refs[4 + len(places) :]
    carried = 2 * sum(not first for _, _, first in plan)
    given, results = refs[:carried], refs[carried:]
    above = where_ref[0]

    for tiles, used, first in plan:
        chunks, spots = [held[k] for k in used], [places[k] for k in used]
        if not first:
            (acc_in, stat_in), given = given[:2], given[2:]
        if last:
            outs = [results[t % 2].at[t // 2] for t in range(4)]
        else:
            (acc_out, stat_out), results = results[:2], results[2:]

        def run(tiles, masked):
            pieces = [(tile, h) for tile in tiles for h in range(heads)]
            spans = [slice(h * DH, (h + 1) * DH) for h in range(heads)]
            scores = [
                [
                    lax.dot_general(
                        chunk[0, :, spans[h]],
                        query_refs[tile][:, spans[h]],
                        (((1,), (1,)), ((), ())),
                        preferred_element_type=F32,
                    )
                    for chunk in chunks
                ]
                for tile, h in pieces
            ]
            if masked:
                drift = lax.broadcasted_iota(jnp.int32, (ROWS, ROWS), 1) - lax.broadcasted_iota(
                    jnp.int32, (ROWS, ROWS), 0
                )
                scores = [
                    [
                        jnp.where(drift >= where_ref[spots[j]] - where_ref[1 + tile], score, HIDDEN)
                        for j, score in enumerate(group)
                    ]
                    for (tile, h), group in zip(pieces, scores)
                ]
            tops = [
                jnp.max(functools.reduce(jnp.maximum, group), axis=0, keepdims=True)
                for group in scores
            ]
            if first:
                tops = [jnp.maximum(top, LOW) for top in tops]
            else:
                old_tops = [stat_in[tile % 2, h : h + 1] for tile, h in pieces]
                tops = [jnp.maximum(top, old) for top, old in zip(tops, old_tops)]
                fades = [jnp.exp2((old - top) * SCALE2) for top, old in zip(tops, old_tops)]
            weights = [
                [jnp.exp2((score - top) * SCALE2) for score in group]
                for group, top in zip(scores, tops)
            ]
            totals = [
                jnp.sum(functools.reduce(jnp.add, group), axis=0, keepdims=True) for group in weights
            ]
            sums = [
                functools.reduce(
                    jnp.add,
                    [
                        jnp.dot(
                            chunk[1, h % 2 * DH : (h % 2 + 1) * DH, h // 2 * ROWS : (h // 2 + 1) * ROWS],
                            weight.astype(BF16),
                            preferred_element_type=F32,
                        )
                        for chunk, weight in zip(chunks, group)
                    ],
                )
                for (tile, h), group in zip(pieces, weights)
            ]
            numbered = {tile: [] for tile in tiles}
            for number, (tile, h) in enumerate(pieces):
                local, span = tile % 2, spans[h]
                top, total, summed = tops[number], totals[number], sums[number]
                if not first:
                    total = total + fades[number] * stat_in[tile % 2, heads + h : heads + h + 1]
                    summed = summed + fades[number] * acc_in[local, span]
                if last:
                    safe = jnp.maximum(total, 1e-30)
                    outs[tile][span] = (summed * (1.0 / safe)).astype(BF16)
                    level = jnp.where(total > 0, top * SCALE2 + jnp.log2(safe), HIDDEN)
                    for k, part in enumerate(exact_parts(level)):
                        numbered[tile].append((k * heads + h, part))
                else:
                    acc_out[local, span] = summed
                    numbered[tile].append((h, top))
                    numbered[tile].append((heads + h, total))
            for tile in tiles:
                if last:
                    outs[tile][heads * DH :] = rows_placed(16, numbered[tile]).astype(BF16)
                else:
                    stat_out[tile % 2] = rows_placed(8, numbered[tile])

        if tiles == NEAR:
            run(tiles, True)
        else:

            @pl.when(above == 0)
            def _():
                run(tiles, False)

            @pl.when(above != 0)
            def _():
                if last:
                    for ref in results:
                        ref[1] = jnp.zeros(ref.shape[1:], BF16)
                else:
                    for ref in (acc_out, stat_out):
                        ref[...] = jnp.zeros(ref.shape, F32)


NEAR, ABOVE = (0, 1), (2, 3)


def attend_call(where, queries, numbered, plan, last=False):
    places, chunks = [3 + number for number, _ in numbered], [chunk for _, chunk in numbered]
    width = queries[2].shape[1]
    heads = width // DH
    operands = [*queries, *chunks, *(array for _, _, state in plan for array in state or ())]
    if last:
        out_shape = tuple(kept((2, width + 16, ROWS), BF16) for _ in range(2))
    else:
        out_shape = tuple(
            kept((2, rows, ROWS), F32) for _ in plan for rows in (width, 8)
        )
    work = 2 * ROWS * ROWS * sum(len(used) for _, used, _ in plan)
    return pl.pallas_call(
        functools.partial(
            attend_kernel,
            places,
            [(tiles, used, state is None) for tiles, used, state in plan],
            last,
            heads,
        ),
        out_shape=out_shape,
        in_specs=[pl.BlockSpec(memory_space=pltpu.SMEM)]
        + [pl.BlockSpec(memory_space=pltpu.VMEM)] * len(operands),
        compiler_params=room(8 + 6 * len(chunks)),
        cost_estimate=pl.CostEstimate(
            flops=4 * work * width,
            bytes_accessed=2 * work * heads,
            transcendentals=work * heads,
        ),
    )(where, *operands)


def levels_of(ref, heads):
    tail = ref[heads * DH :].astype(F32)
    return tail[:heads] + tail[heads : 2 * heads] + tail[2 * heads : 3 * heads]


def shares_of(levels):
    top = functools.reduce(jnp.maximum, levels)
    shares = [jnp.exp2(level - top) for level in levels]
    total = functools.reduce(jnp.add, shares)
    return [share / total for share in shares], top + jnp.log2(total)


def blended(refs, shares, h):
    span = slice(h * DH, (h + 1) * DH)
    return functools.reduce(
        jnp.add, [ref[span].astype(F32) * share[h : h + 1] for ref, share in zip(refs, shares)]
    )


def merge_kernel(heads, a_ref, b_ref, o_ref):
    refs = (a_ref.at[1], b_ref.at[1])
    shares, level = shares_of([levels_of(ref, heads) for ref in refs])
    for h in range(heads):
        o_ref[h * DH : (h + 1) * DH] = blended(refs, shares, h).astype(BF16)
    parts = [
        (k * heads + h, part[h : h + 1])
        for k, part in enumerate(exact_parts(level))
        for h in range(heads)
    ]
    o_ref[heads * DH :] = rows_placed(16, parts).astype(BF16)


def merge_call(a, b):
    heads = a.shape[1] // DH
    return pl.pallas_call(
        functools.partial(merge_kernel, heads),
        out_shape=kept(a.shape[1:], BF16),
        compiler_params=room(8),
    )(a, b)


def combine_kernel(heads, where_ref, a_ref, b_ref, s_ref, att_ref, square_ref):
    refs = (a_ref.at[0], b_ref.at[0], s_ref)
    levels = [levels_of(ref, heads) for ref in refs]
    levels[2] = jnp.where(where_ref[0] != 0, levels[2], HIDDEN)
    shares, _ = shares_of(levels)
    squares = jnp.zeros((DH, ROWS), F32)
    for h in range(heads):
        half = blended(refs, shares, h).astype(BF16)
        att_ref[h * DH : (h + 1) * DH] = half
        wide = half.astype(F32)
        squares = squares + wide * wide
    square_ref[...] = jnp.broadcast_to(
        jnp.sum(squares, axis=0, keepdims=True)[None], square_ref.shape
    )


def combine_call(where, a, b, s, group):
    heads = s.shape[0] // DH
    return pl.pallas_call(
        functools.partial(combine_kernel, heads),
        out_shape=(
            kept((heads * DH, ROWS), BF16),
            kept((group, 1, ROWS), F32),
        ),
        in_specs=[pl.BlockSpec(memory_space=pltpu.SMEM)]
        + [pl.BlockSpec(memory_space=pltpu.VMEM)] * 3,
        compiler_params=room(8),
    )(where, a, b, s)


def turn_kernel(heads, att_ref, gain_ref, o_ref):
    for h in range(heads):
        span = slice(h * DH, (h + 1) * DH)
        o_ref[:, span] = att_ref[span].astype(F32).T * gain_ref[:, span]


def turn_call(attention, gain):
    return pl.pallas_call(
        functools.partial(turn_kernel, attention.shape[0] // DH),
        out_shape=kept(attention.shape[::-1], F32),
        compiler_params=room(8),
    )(attention, gain.reshape(1, -1))


def finish_kernel(heads, spread_ref, wide_ref, hyena_ref, o_ref):
    factor = lax.rsqrt(jnp.sum(spread_ref[...], axis=0) / WIDTH + 1e-06)
    factor = jnp.broadcast_to(factor, (DH, ROWS)).T
    for h in range(heads):
        span = slice(h * DH, (h + 1) * DH)
        o_ref[:, span] = (wide_ref[:, span] * factor + hyena_ref[:, span]).astype(BF16)


def finish_call(spread, wide, hyena_out):
    return pl.pallas_call(
        functools.partial(finish_kernel, wide.shape[1] // DH),
        out_shape=jax.ShapeDtypeStruct(wide.shape, BF16),
        compiler_params=room(8),
    )(spread, wide, hyena_out)


def gate_kernel(rim_ref, input_ref, filter_ref, o_ref, product):
    rim_rows = rim_ref.shape[1]
    product[8 - rim_rows : 8] = rim_ref[0].astype(F32) * rim_ref[1].astype(F32)
    product[8:] = input_ref[1].astype(F32) * input_ref[2].astype(F32)
    convolved = filter_ref[0:1] * product[8:]
    for tap in range(1, rim_rows + 1):
        convolved = convolved + filter_ref[tap : tap + 1] * product[8 - tap : 8 - tap + ROWS]
    o_ref[...] = input_ref[0].astype(F32) * convolved


def gate_call(rim, hyena_inputs, hyena_filter):
    width = hyena_filter.shape[1]
    return pl.pallas_call(
        gate_kernel,
        out_shape=kept((ROWS, width), F32),
        scratch_shapes=[pltpu.VMEM((8 + ROWS, width), F32)],
        compiler_params=room(8),
    )(rim, hyena_inputs, hyena_filter)


def rim_of(hyena_inputs, rim_rows):
    tails = hyena_inputs[1:, hyena_inputs.shape[1] - rim_rows :, :]
    size = lax.axis_size("ctx")
    return lax.ppermute(tails, "ctx", [(i, i + 1) for i in range(size - 1)])


def on_device(queries, keys, values, hyena_inputs, hyena_filter, norm_gain):
    ctx = lax.axis_index("ctx")
    x, z, c = ctx // (2 * Z), (ctx // 2) % Z, ctx % 2
    toward = 2 * c - 1
    own, own_all = prepare_call(keys, values, queries)
    other = lax.ppermute(own_all, "ctx", CORES)
    ring = lambda chunk: lax.ppermute(chunk, "ctx", RING)
    after = lambda chunk, token: lax.optimization_barrier((chunk, token))

    same, near_row, far_row = z * 2 * ROWS, c * ROWS, (1 - c) * ROWS
    blocks = [((z + step * toward) % Z) * 2 * ROWS for step in range(5)]
    where = jnp.stack(
        [x, same + near_row, same + far_row]
        + [block + near_row for block in blocks]
        + [block + far_row for block in blocks]
    ).astype(jnp.int32)

    above = lax.ppermute(queries, "ctx", DOWN)
    rim = rim_of(hyena_inputs, hyena_filter.shape[0] - 1)
    a0, b0 = own, other[:2]
    a1, b1 = ring(a0), ring(b0)
    a2, b2 = ring(a1), ring(b1)
    near = attend_call(
        where,
        (own_all, other, queries, queries),
        [(0, a0), (1, a1), (6, b1)],
        [(NEAR, (0, 1, 2), None)],
    )
    a2, stat, above, rim = lax.optimization_barrier((a2, near[1], above, rim))
    near = (near[0], stat)
    queries_all = (own_all, other, above, lax.ppermute(above, "ctx", CORES))
    a3, b3 = ring(a2), ring(b2)
    acc, stat = attend_call(
        where,
        queries_all,
        [(0, a0), (1, a1), (6, b1)],
        [(ABOVE, (0, 1, 2), None)],
    )
    a3, stat = after(a3, stat)
    a4 = ring(a3)
    *near, acc, stat = attend_call(
        where,
        queries_all,
        [(2, a2), (7, b2), (3, a3), (8, b3)],
        [(NEAR, (0, 1, 2, 3), near), (ABOVE, (0, 1, 2, 3), (acc, stat))],
    )
    near, far = attend_call(
        where,
        queries_all,
        [(4, a4)],
        [(NEAR, (0,), near), (ABOVE, (0,), (acc, stat))],
        True,
    )
    crossed = lax.ppermute(far, "ctx", CORES)
    rim, below = after(rim, merge_call(near, crossed))
    gate = gate_call(rim, hyena_inputs, hyena_filter)
    across = lax.ppermute(below, "ctx", UP)
    group = lax.axis_size("heads")
    attention, squares = combine_call(
        where, near, crossed, across, group
    )
    spread = lax.all_to_all(squares, "heads", 0, 0, tiled=True)
    wide = turn_call(attention, norm_gain)
    return finish_call(spread, wide, gate)


def solution(mesh):
    placed = (
        P("ctx", "heads"),
        P("ctx", "heads"),
        P("ctx", "heads"),
        P(None, "ctx", "heads"),
        P(None, "heads"),
        P("heads"),
    )
    return jax.shard_map(
        on_device, mesh=mesh, in_specs=placed, out_specs=P("ctx", "heads"), check_vma=False
    )
```

```python
import functools
import math

import jax
import jax.numpy as jnp
from jax import lax
from jax.experimental import pallas as pl
from jax.experimental.pallas import tpu as pltpu
from jax.sharding import PartitionSpec as P

DH = 128
WIDTH = 8192
Z = 8
ROWS = 256
SCALE2 = math.log2(math.e) / math.sqrt(DH)
LOW = -1e29
HIDDEN = -1e30
F32 = jnp.float32
BF16 = jnp.bfloat16


def chip(x, z, c):
    return (x * Z + z % Z) * 2 + c


RING = [
    (chip(x, z, c), chip(x, z + 1 - 2 * c, c)) for x in range(2) for z in range(Z) for c in range(2)
]
CORES = [(chip(x, z, c), chip(x, z, 1 - c)) for x in range(2) for z in range(Z) for c in range(2)]
DOWN = [(chip(1, z, c), chip(0, z, c)) for z in range(Z) for c in range(2)]
CROSS = [(chip(1, z, c), chip(0, z, 1 - c)) for z in range(Z) for c in range(2)]
UP = [(chip(0, z, c), chip(1, z, c)) for z in range(Z) for c in range(2)]


def kept(shape, dtype):
    return pltpu.VMEM(shape, dtype)


def room(mebibytes):
    return pltpu.CompilerParams(vmem_limit_bytes=mebibytes * 1024 * 1024)


def rows_placed(count, numbered):
    row = lax.broadcasted_iota(jnp.int32, (count, ROWS), 0)
    result = jnp.zeros((count, ROWS), F32)
    for number, value in numbered:
        result = jnp.where(row == number, value, result)
    return result


def exact_parts(value):
    high = value.astype(BF16).astype(F32)
    rest = value - high
    middle = rest.astype(BF16).astype(F32)
    return high, middle, rest - middle


def corner(h):
    return slice(h % 2 * DH, (h % 2 + 1) * DH), slice(h // 2 * ROWS, (h // 2 + 1) * ROWS)


def prepare_kernel(heads, k_ref, v_ref, q_ref, pair_ref, triple_ref, turned_ref, held, sems):
    copies = [
        pltpu.make_async_copy(source, target, sems.at[number])
        for number, (source, target) in enumerate(
            (
                (v_ref, held.at[0]),
                (q_ref, held.at[1]),
                (k_ref, pair_ref.at[0]),
                (k_ref, triple_ref.at[0]),
            )
        )
    ]
    for copy in copies:
        copy.start()
    for number, refs in enumerate(
        ((pair_ref.at[1], triple_ref.at[1]), (triple_ref.at[2], turned_ref))
    ):
        copies[number].wait()
        for h in range(heads):
            turned = held[number, :, h * DH : (h + 1) * DH].T
            for ref in refs:
                ref[corner(h)] = turned
    for copy in copies[2:]:
        copy.wait()


def prepare_call(keys, values, queries):
    return pl.pallas_call(
        functools.partial(prepare_kernel, keys.shape[1] // DH),
        out_shape=(
            *(kept((n, *keys.shape), BF16) for n in (2, 3)),
            kept(queries.shape, BF16),
        ),
        in_specs=[pl.BlockSpec(memory_space=pl.ANY)] * 3,
        scratch_shapes=[pltpu.VMEM((2, *values.shape), BF16), pltpu.SemaphoreType.DMA((4,))],
        compiler_params=room(56),
    )(keys, values, queries)


def attend_kernel(places, plan, last, heads, where_ref, *refs):
    query_refs = (refs[0].at[2], refs[1].at[2], refs[2], refs[3])
    held = refs[4 : 4 + len(places)]
    refs = refs[4 + len(places) :]
    carried = 2 * sum(not first for _, _, first in plan)
    given, results = refs[:carried], refs[carried:]
    above = where_ref[0]

    for tiles, used, first in plan:
        chunks, spots = [held[k] for k in used], [places[k] for k in used]
        if not first:
            (acc_in, stat_in), given = given[:2], given[2:]
        if last:
            outs = [results[t % 2].at[t // 2] for t in range(4)]
        else:
            (acc_out, stat_out), results = results[:2], results[2:]

        def run(tiles, masked):
            pieces = [(tile, h) for tile in tiles for h in range(heads)]
            spans = [slice(h * DH, (h + 1) * DH) for h in range(heads)]
            scores = [
                [
                    jnp.dot(
                        chunk[0, :, spans[h]],
                        query_refs[tile][corner(h)],
                        preferred_element_type=F32,
                    )
                    for chunk in chunks
                ]
                for tile, h in pieces
            ]
            if masked:
                drift = lax.broadcasted_iota(jnp.int32, (ROWS, ROWS), 1) - lax.broadcasted_iota(
                    jnp.int32, (ROWS, ROWS), 0
                )
                scores = [
                    [
                        jnp.where(drift >= where_ref[spots[j]] - where_ref[1 + tile], score, HIDDEN)
                        for j, score in enumerate(group)
                    ]
                    for (tile, h), group in zip(pieces, scores)
                ]
            tops = [
                jnp.max(functools.reduce(jnp.maximum, group), axis=0, keepdims=True)
                for group in scores
            ]
            if first:
                tops = [jnp.maximum(top, LOW) for top in tops]
            else:
                old_tops = [stat_in[tile % 2, h : h + 1] for tile, h in pieces]
                tops = [jnp.maximum(top, old) for top, old in zip(tops, old_tops)]
                fades = [jnp.exp2((old - top) * SCALE2) for top, old in zip(tops, old_tops)]
            weights = [
                [jnp.exp2((score - top) * SCALE2) for score in group]
                for group, top in zip(scores, tops)
            ]
            totals = [
                jnp.sum(functools.reduce(jnp.add, group), axis=0, keepdims=True) for group in weights
            ]
            sums = [
                functools.reduce(
                    jnp.add,
                    [
                        jnp.dot(
                            chunk[(1, *corner(h))],
                            weight.astype(BF16),
                            preferred_element_type=F32,
                        )
                        for chunk, weight in zip(chunks, group)
                    ],
                )
                for (tile, h), group in zip(pieces, weights)
            ]
            numbered = {tile: [] for tile in tiles}
            for number, (tile, h) in enumerate(pieces):
                local, span = tile % 2, spans[h]
                top, total, summed = tops[number], totals[number], sums[number]
                if not first:
                    total = total + fades[number] * stat_in[tile % 2, heads + h : heads + h + 1]
                    summed = summed + fades[number] * acc_in[local, span]
                if last:
                    safe = jnp.maximum(total, 1e-30)
                    outs[tile][span] = (summed * (1.0 / safe)).astype(BF16)
                    level = jnp.where(total > 0, top * SCALE2 + jnp.log2(safe), HIDDEN)
                    for k, part in enumerate(exact_parts(level)):
                        numbered[tile].append((k * heads + h, part))
                else:
                    acc_out[local, span] = summed
                    numbered[tile].append((h, top))
                    numbered[tile].append((heads + h, total))
            for tile in tiles:
                if last:
                    outs[tile][heads * DH :] = rows_placed(16, numbered[tile]).astype(BF16)
                else:
                    stat_out[tile % 2] = rows_placed(8, numbered[tile])

        if tiles == NEAR:
            run(tiles, True)
        else:

            @pl.when(above == 0)
            def _():
                run(tiles, False)

            @pl.when(above != 0)
            def _():
                if last:
                    for ref in results:
                        ref[1] = jnp.zeros(ref.shape[1:], BF16)
                else:
                    for ref in (acc_out, stat_out):
                        ref[...] = jnp.zeros(ref.shape, F32)


NEAR, ABOVE = (0, 1), (2, 3)


def attend_call(where, queries, numbered, plan, last=False):
    places, chunks = [3 + number for number, _ in numbered], [chunk for _, chunk in numbered]
    width = queries[2].shape[1]
    heads = width // DH
    operands = [*queries, *chunks, *(array for _, _, state in plan for array in state or ())]
    if last:
        out_shape = tuple(kept((2, width + 16, ROWS), BF16) for _ in range(2))
    else:
        out_shape = tuple(
            kept((2, rows, ROWS), F32) for _ in plan for rows in (width, 8)
        )
    work = 2 * ROWS * ROWS * sum(len(used) for _, used, _ in plan)
    return pl.pallas_call(
        functools.partial(
            attend_kernel,
            places,
            [(tiles, used, state is None) for tiles, used, state in plan],
            last,
            heads,
        ),
        out_shape=out_shape,
        in_specs=[pl.BlockSpec(memory_space=pltpu.SMEM)]
        + [pl.BlockSpec(memory_space=pltpu.VMEM)] * len(operands),
        compiler_params=room(8 + 6 * len(chunks)),
        cost_estimate=pl.CostEstimate(
            flops=4 * work * width,
            bytes_accessed=2 * work * heads,
            transcendentals=work * heads,
        ),
    )(where, *operands)


def levels_of(ref, heads):
    tail = ref[heads * DH :].astype(F32)
    return tail[:heads] + tail[heads : 2 * heads] + tail[2 * heads : 3 * heads]


def shares_of(levels):
    top = functools.reduce(jnp.maximum, levels)
    shares = [jnp.exp2(level - top) for level in levels]
    total = functools.reduce(jnp.add, shares)
    return [share / total for share in shares], top + jnp.log2(total)


def blended(refs, shares, h):
    span = slice(h * DH, (h + 1) * DH)
    return functools.reduce(
        jnp.add, [ref[span].astype(F32) * share[h : h + 1] for ref, share in zip(refs, shares)]
    )


def merge_kernel(heads, a_ref, b_ref, o_ref):
    refs = (a_ref.at[1], b_ref.at[1])
    shares, level = shares_of([levels_of(ref, heads) for ref in refs])
    for h in range(heads):
        o_ref[h * DH : (h + 1) * DH] = blended(refs, shares, h).astype(BF16)
    parts = [
        (k * heads + h, part[h : h + 1])
        for k, part in enumerate(exact_parts(level))
        for h in range(heads)
    ]
    o_ref[heads * DH :] = rows_placed(16, parts).astype(BF16)


def merge_call(a, b):
    heads = a.shape[1] // DH
    return pl.pallas_call(
        functools.partial(merge_kernel, heads),
        out_shape=kept(a.shape[1:], BF16),
        compiler_params=room(8),
    )(a, b)


def combine_kernel(heads, where_ref, a_ref, b_ref, s_ref, att_ref, square_ref):
    refs = (a_ref.at[0], b_ref.at[0], s_ref)
    levels = [levels_of(ref, heads) for ref in refs]
    levels[2] = jnp.where(where_ref[0] != 0, levels[2], HIDDEN)
    shares, _ = shares_of(levels)
    squares = jnp.zeros((DH, ROWS), F32)
    for h in range(heads):
        half = blended(refs, shares, h).astype(BF16)
        att_ref[h * DH : (h + 1) * DH] = half
        wide = half.astype(F32)
        squares = squares + wide * wide
    square_ref[...] = jnp.broadcast_to(
        jnp.sum(squares, axis=0, keepdims=True)[None], square_ref.shape
    )


def combine_call(where, a, b, s, group):
    heads = s.shape[0] // DH
    return pl.pallas_call(
        functools.partial(combine_kernel, heads),
        out_shape=(
            kept((heads * DH, ROWS), BF16),
            kept((group, 1, ROWS), F32),
        ),
        in_specs=[pl.BlockSpec(memory_space=pltpu.SMEM)]
        + [pl.BlockSpec(memory_space=pltpu.VMEM)] * 3,
        compiler_params=room(8),
    )(where, a, b, s)


def turn_kernel(heads, att_ref, gain_ref, o_ref):
    for h in range(heads):
        span = slice(h * DH, (h + 1) * DH)
        o_ref[:, span] = att_ref[span].astype(F32).T * gain_ref[:, span]


def turn_call(attention, gain):
    return pl.pallas_call(
        functools.partial(turn_kernel, attention.shape[0] // DH),
        out_shape=kept(attention.shape[::-1], F32),
        compiler_params=room(8),
    )(attention, gain)


def finish_kernel(heads, spread_ref, wide_ref, hyena_ref, o_ref):
    factor = lax.rsqrt(jnp.sum(spread_ref[...], axis=0) / WIDTH + 1e-06)
    factor = jnp.broadcast_to(factor, (DH, ROWS)).T
    for h in range(heads):
        span = slice(h * DH, (h + 1) * DH)
        o_ref[:, span] = (wide_ref[:, span] * factor + hyena_ref[:, span]).astype(BF16)


def finish_call(spread, wide, hyena_out):
    return pl.pallas_call(
        functools.partial(finish_kernel, wide.shape[1] // DH),
        out_shape=jax.ShapeDtypeStruct(wide.shape, BF16),
        compiler_params=room(8),
    )(spread, wide, hyena_out)


def gate_kernel(rim_ref, input_ref, filter_ref, gain_ref, o_ref, gain_out, product):
    gain_out[...] = gain_ref[...]
    rim_rows = rim_ref.shape[1]
    product[8 - rim_rows : 8] = rim_ref[0].astype(F32) * rim_ref[1].astype(F32)
    product[8:] = input_ref[1].astype(F32) * input_ref[2].astype(F32)
    convolved = filter_ref[0:1] * product[8:]
    for tap in range(1, rim_rows + 1):
        convolved = convolved + filter_ref[tap : tap + 1] * product[8 - tap : 8 - tap + ROWS]
    o_ref[...] = input_ref[0].astype(F32) * convolved


def gate_call(rim, hyena_inputs, hyena_filter, gain):
    width = hyena_filter.shape[1]
    return pl.pallas_call(
        gate_kernel,
        out_shape=(kept((ROWS, width), F32), kept((1, width), F32)),
        scratch_shapes=[pltpu.VMEM((8 + ROWS, width), F32)],
        compiler_params=room(8),
    )(rim, hyena_inputs, hyena_filter, gain.reshape(1, -1))


def rim_of(tails):
    size = lax.axis_size("ctx")
    return lax.ppermute(tails, "ctx", [(i, i + 1) for i in range(size - 1)])


def on_device(queries, keys, values, hyena_inputs, hyena_filter, norm_gain):
    ctx = lax.axis_index("ctx")
    x, z, c = ctx // (2 * Z), (ctx // 2) % Z, ctx % 2
    toward = 2 * c - 1
    own, own_all, turned = prepare_call(keys, values, queries)
    other = lax.ppermute(own_all, "ctx", CORES)
    ring = lambda chunk: lax.ppermute(chunk, "ctx", RING)
    after = lambda chunk, token: lax.optimization_barrier((chunk, token))

    same, near_row, far_row = z * 2 * ROWS, c * ROWS, (1 - c) * ROWS
    blocks = [((z + step * toward) % Z) * 2 * ROWS for step in range(5)]
    where = jnp.stack(
        [x, same + near_row, same + far_row]
        + [block + near_row for block in blocks]
        + [block + far_row for block in blocks]
    ).astype(jnp.int32)

    queries_near = (own_all, other, turned, turned)
    above = lax.ppermute(turned, "ctx", DOWN)
    a0, b0 = own, other[:2]
    a1, b1 = ring(a0), ring(b0)
    acc, stat = attend_call(where, queries_near, [(0, a0)], [(NEAR, (0,), None)])
    a1, stat, above = lax.optimization_barrier((a1, stat, above))
    queries_all = (own_all, other, above, lax.ppermute(above, "ctx", CORES))
    a2 = ring(a1)
    acc, stat = attend_call(where, queries_near, [(1, a1)], [(NEAR, (0,), (acc, stat))])
    b1, stat = after(b1, stat)
    b2 = ring(b1)
    high = attend_call(where, queries_all, [(0, a0), (1, a1)], [(ABOVE, (0, 1), None)])
    a2, mark = after(a2, high[1])
    a3, b3 = ring(a2), ring(b2)
    near = attend_call(
        where,
        queries_near,
        [(6, b1), (2, a2), (7, b2)],
        [(NEAR, (0, 1, 2), (acc, stat))],
    )
    a3, stat = after(a3, near[1])
    a4 = ring(a3)
    *near, acc, stat = attend_call(
        where,
        queries_all,
        [(6, b1), (2, a2), (7, b2), (3, a3), (8, b3)],
        [(NEAR, (3, 4), (near[0], stat)), (ABOVE, (0, 1, 2, 3, 4), (high[0], mark))],
    )
    near, far = attend_call(
        where,
        queries_all,
        [(4, a4)],
        [(NEAR, (0,), near), (ABOVE, (0,), (acc, stat))],
        True,
    )
    crossed = lax.ppermute(far, "ctx", CORES)
    tails = hyena_inputs[1:, ROWS - hyena_filter.shape[0] + 1 :, :]
    tails, below = after(tails, merge_call(near, crossed))
    rim = rim_of(tails)
    gate, gain = gate_call(rim, hyena_inputs, hyena_filter, norm_gain)
    across, gain = after(lax.ppermute(below, "ctx", UP), gain)
    group = lax.axis_size("heads")
    attention, squares = combine_call(
        where, near, crossed, across, group
    )
    spread = lax.all_to_all(squares, "heads", 0, 0, tiled=True)
    wide = turn_call(attention, gain)
    return finish_call(spread, wide, gate)


def solution(mesh):
    placed = (
        P("ctx", "heads"),
        P("ctx", "heads"),
        P("ctx", "heads"),
        P(None, "ctx", "heads"),
        P(None, "heads"),
        P("heads"),
    )
    return jax.shard_map(
        on_device, mesh=mesh, in_specs=placed, out_specs=P("ctx", "heads"), check_vma=False
    )
```

```python
import functools
import math

import jax
import jax.numpy as jnp
from jax import lax
from jax.experimental import pallas as pl
from jax.experimental.pallas import tpu as pltpu
from jax.sharding import PartitionSpec as P

DH = 128
WIDTH = 8192
Z = 8
ROWS = 256
SCALE2 = math.log2(math.e) / math.sqrt(DH)
LOW = -1e29
HIDDEN = -1e30
F32 = jnp.float32
BF16 = jnp.bfloat16


def chip(x, z, c):
    return (x * Z + z % Z) * 2 + c


RING = [
    (chip(x, z, c), chip(x, z + 1 - 2 * c, c)) for x in range(2) for z in range(Z) for c in range(2)
]
CORES = [(chip(x, z, c), chip(x, z, 1 - c)) for x in range(2) for z in range(Z) for c in range(2)]
DOWN = [(chip(1, z, c), chip(0, z, c)) for z in range(Z) for c in range(2)]
CROSS = [(chip(1, z, c), chip(0, z, 1 - c)) for z in range(Z) for c in range(2)]
UP = [(chip(0, z, c), chip(1, z, c)) for z in range(Z) for c in range(2)]


def kept(shape, dtype):
    return pltpu.VMEM(shape, dtype)


def room(mebibytes):
    return pltpu.CompilerParams(vmem_limit_bytes=mebibytes * 1024 * 1024)


def rows_placed(count, numbered):
    row = lax.broadcasted_iota(jnp.int32, (count, ROWS), 0)
    result = jnp.zeros((count, ROWS), F32)
    for number, value in numbered:
        result = jnp.where(row == number, value, result)
    return result


def exact_parts(value):
    high = value.astype(BF16).astype(F32)
    rest = value - high
    middle = rest.astype(BF16).astype(F32)
    return high, middle, rest - middle


def corner(h):
    return slice(h % 2 * DH, (h % 2 + 1) * DH), slice(h // 2 * ROWS, (h // 2 + 1) * ROWS)


def prepare_kernel(heads, k_ref, v_ref, q_ref, pair_ref, triple_ref, turned_ref, held, sems):
    copies = [
        pltpu.make_async_copy(source, target, sems.at[number])
        for number, (source, target) in enumerate(
            (
                (v_ref, held.at[0]),
                (q_ref, held.at[1]),
                (k_ref, pair_ref.at[0]),
                (k_ref, triple_ref.at[0]),
            )
        )
    ]
    for copy in copies:
        copy.start()
    for number, refs in enumerate(
        ((pair_ref.at[1], triple_ref.at[1]), (triple_ref.at[2], turned_ref))
    ):
        copies[number].wait()
        for h in range(heads):
            turned = held[number, :, h * DH : (h + 1) * DH].T
            for ref in refs:
                ref[corner(h)] = turned
    for copy in copies[2:]:
        copy.wait()


def prepare_call(keys, values, queries):
    return pl.pallas_call(
        functools.partial(prepare_kernel, keys.shape[1] // DH),
        out_shape=(
            *(kept((n, *keys.shape), BF16) for n in (2, 3)),
            kept(queries.shape, BF16),
        ),
        in_specs=[pl.BlockSpec(memory_space=pl.ANY)] * 3,
        scratch_shapes=[pltpu.VMEM((2, *values.shape), BF16), pltpu.SemaphoreType.DMA((4,))],
        compiler_params=room(56),
    )(keys, values, queries)


def attend_kernel(places, plan, last, heads, where_ref, *refs):
    query_refs = (refs[0].at[2], refs[1].at[2], refs[2], refs[3])
    held = refs[4 : 4 + len(places)]
    refs = refs[4 + len(places) :]
    carried = 2 * sum(not first for _, _, first in plan)
    given, results = refs[:carried], refs[carried:]
    above = where_ref[0]

    for tiles, used, first in plan:
        chunks, spots = [held[k] for k in used], [places[k] for k in used]
        if not first:
            (acc_in, stat_in), given = given[:2], given[2:]
        if last:
            outs = [results[t % 2].at[t // 2] for t in range(4)]
        else:
            (acc_out, stat_out), results = results[:2], results[2:]

        def run(tiles, masked):
            pieces = [(tile, h) for tile in tiles for h in range(heads)]
            spans = [slice(h * DH, (h + 1) * DH) for h in range(heads)]
            scores = [
                [
                    jnp.dot(
                        chunk[0, :, spans[h]],
                        query_refs[tile][corner(h)],
                        preferred_element_type=F32,
                    )
                    for chunk in chunks
                ]
                for tile, h in pieces
            ]
            if masked:
                drift = lax.broadcasted_iota(jnp.int32, (ROWS, ROWS), 1) - lax.broadcasted_iota(
                    jnp.int32, (ROWS, ROWS), 0
                )
                scores = [
                    [
                        jnp.where(drift >= where_ref[spots[j]] - where_ref[1 + tile], score, HIDDEN)
                        for j, score in enumerate(group)
                    ]
                    for (tile, h), group in zip(pieces, scores)
                ]
            tops = [
                jnp.max(functools.reduce(jnp.maximum, group), axis=0, keepdims=True)
                for group in scores
            ]
            if first:
                tops = [jnp.maximum(top, LOW) for top in tops]
            else:
                old_tops = [stat_in[tile % 2, h : h + 1] for tile, h in pieces]
                tops = [jnp.maximum(top, old) for top, old in zip(tops, old_tops)]
                fades = [jnp.exp2((old - top) * SCALE2) for top, old in zip(tops, old_tops)]
            weights = [
                [jnp.exp2((score - top) * SCALE2) for score in group]
                for group, top in zip(scores, tops)
            ]
            totals = [
                jnp.sum(functools.reduce(jnp.add, group), axis=0, keepdims=True) for group in weights
            ]
            sums = [
                functools.reduce(
                    jnp.add,
                    [
                        jnp.dot(
                            chunk[(1, *corner(h))],
                            weight.astype(BF16),
                            preferred_element_type=F32,
                        )
                        for chunk, weight in zip(chunks, group)
                    ],
                )
                for (tile, h), group in zip(pieces, weights)
            ]
            numbered = {tile: [] for tile in tiles}
            for number, (tile, h) in enumerate(pieces):
                local, span = tile % 2, spans[h]
                top, total, summed = tops[number], totals[number], sums[number]
                if not first:
                    total = total + fades[number] * stat_in[tile % 2, heads + h : heads + h + 1]
                    summed = summed + fades[number] * acc_in[local, span]
                if last:
                    safe = jnp.maximum(total, 1e-30)
                    outs[tile][span] = (summed * (1.0 / safe)).astype(BF16)
                    level = jnp.where(total > 0, top * SCALE2 + jnp.log2(safe), HIDDEN)
                    for k, part in enumerate(exact_parts(level)):
                        numbered[tile].append((k * heads + h, part))
                else:
                    acc_out[local, span] = summed
                    numbered[tile].append((h, top))
                    numbered[tile].append((heads + h, total))
            for tile in tiles:
                if last:
                    outs[tile][heads * DH :] = rows_placed(16, numbered[tile]).astype(BF16)
                else:
                    stat_out[tile % 2] = rows_placed(8, numbered[tile])

        if tiles == NEAR:
            run(tiles, True)
        else:

            @pl.when(above == 0)
            def _():
                run(tiles, False)

            @pl.when(above != 0)
            def _():
                if last:
                    for ref in results:
                        ref[1] = jnp.zeros(ref.shape[1:], BF16)
                else:
                    for ref in (acc_out, stat_out):
                        ref[...] = jnp.zeros(ref.shape, F32)


NEAR, ABOVE = (0, 1), (2, 3)


def attend_call(where, queries, numbered, plan, last=False):
    places, chunks = [3 + number for number, _ in numbered], [chunk for _, chunk in numbered]
    width = queries[2].shape[1]
    heads = width // DH
    operands = [*queries, *chunks, *(array for _, _, state in plan for array in state or ())]
    if last:
        out_shape = tuple(kept((2, width + 16, ROWS), BF16) for _ in range(2))
    else:
        out_shape = tuple(
            kept((2, rows, ROWS), F32) for _ in plan for rows in (width, 8)
        )
    work = 2 * ROWS * ROWS * sum(len(used) for _, used, _ in plan)
    return pl.pallas_call(
        functools.partial(
            attend_kernel,
            places,
            [(tiles, used, state is None) for tiles, used, state in plan],
            last,
            heads,
        ),
        out_shape=out_shape,
        in_specs=[pl.BlockSpec(memory_space=pltpu.SMEM)]
        + [pl.BlockSpec(memory_space=pltpu.VMEM)] * len(operands),
        compiler_params=room(8 + 6 * len(chunks)),
        cost_estimate=pl.CostEstimate(
            flops=4 * work * width,
            bytes_accessed=2 * work * heads,
            transcendentals=work * heads,
        ),
    )(where, *operands)


def levels_of(ref, heads):
    tail = ref[heads * DH :].astype(F32)
    return tail[:heads] + tail[heads : 2 * heads] + tail[2 * heads : 3 * heads]


def shares_of(levels):
    top = functools.reduce(jnp.maximum, levels)
    shares = [jnp.exp2(level - top) for level in levels]
    total = functools.reduce(jnp.add, shares)
    return [share / total for share in shares], top + jnp.log2(total)


def blended(refs, shares, h):
    span = slice(h * DH, (h + 1) * DH)
    return functools.reduce(
        jnp.add, [ref[span].astype(F32) * share[h : h + 1] for ref, share in zip(refs, shares)]
    )


def merge_kernel(heads, a_ref, b_ref, o_ref):
    refs = (a_ref.at[1], b_ref.at[1])
    shares, level = shares_of([levels_of(ref, heads) for ref in refs])
    for h in range(heads):
        o_ref[h * DH : (h + 1) * DH] = blended(refs, shares, h).astype(BF16)
    parts = [
        (k * heads + h, part[h : h + 1])
        for k, part in enumerate(exact_parts(level))
        for h in range(heads)
    ]
    o_ref[heads * DH :] = rows_placed(16, parts).astype(BF16)


def merge_call(a, b):
    heads = a.shape[1] // DH
    return pl.pallas_call(
        functools.partial(merge_kernel, heads),
        out_shape=kept(a.shape[1:], BF16),
        compiler_params=room(8),
    )(a, b)


def combine_kernel(heads, where_ref, a_ref, b_ref, s_ref, att_ref, square_ref):
    refs = (a_ref.at[0], b_ref.at[0], s_ref)
    levels = [levels_of(ref, heads) for ref in refs]
    levels[2] = jnp.where(where_ref[0] != 0, levels[2], HIDDEN)
    shares, _ = shares_of(levels)
    squares = jnp.zeros((DH, ROWS), F32)
    for h in range(heads):
        half = blended(refs, shares, h).astype(BF16)
        att_ref[h * DH : (h + 1) * DH] = half
        wide = half.astype(F32)
        squares = squares + wide * wide
    square_ref[...] = jnp.broadcast_to(
        jnp.sum(squares, axis=0, keepdims=True)[None], square_ref.shape
    )


def combine_call(where, a, b, s, group):
    heads = s.shape[0] // DH
    return pl.pallas_call(
        functools.partial(combine_kernel, heads),
        out_shape=(
            kept((heads * DH, ROWS), BF16),
            kept((group, 1, ROWS), F32),
        ),
        in_specs=[pl.BlockSpec(memory_space=pltpu.SMEM)]
        + [pl.BlockSpec(memory_space=pltpu.VMEM)] * 3,
        compiler_params=room(8),
    )(where, a, b, s)


def turn_kernel(heads, att_ref, gain_ref, o_ref):
    for h in range(heads):
        span = slice(h * DH, (h + 1) * DH)
        o_ref[:, span] = att_ref[span].astype(F32).T * gain_ref[:, span]


def turn_call(attention, gain):
    return pl.pallas_call(
        functools.partial(turn_kernel, attention.shape[0] // DH),
        out_shape=kept(attention.shape[::-1], F32),
        compiler_params=room(8),
    )(attention, gain)


def finish_kernel(heads, spread_ref, wide_ref, hyena_ref, o_ref):
    factor = lax.rsqrt(jnp.sum(spread_ref[...], axis=0) / WIDTH + 1e-06)
    factor = jnp.broadcast_to(factor, (DH, ROWS)).T
    for h in range(heads):
        span = slice(h * DH, (h + 1) * DH)
        o_ref[:, span] = (wide_ref[:, span] * factor + hyena_ref[:, span]).astype(BF16)


def finish_call(spread, wide, hyena_out):
    return pl.pallas_call(
        functools.partial(finish_kernel, wide.shape[1] // DH),
        out_shape=jax.ShapeDtypeStruct(wide.shape, BF16),
        compiler_params=room(8),
    )(spread, wide, hyena_out)


def gate_kernel(rim_ref, input_ref, filter_ref, gain_ref, o_ref, gain_out, product):
    gain_out[...] = gain_ref[...]
    rim_rows = rim_ref.shape[1]
    product[8 - rim_rows : 8] = rim_ref[0].astype(F32) * rim_ref[1].astype(F32)
    product[8:] = input_ref[1].astype(F32) * input_ref[2].astype(F32)
    convolved = filter_ref[0:1] * product[8:]
    for tap in range(1, rim_rows + 1):
        convolved = convolved + filter_ref[tap : tap + 1] * product[8 - tap : 8 - tap + ROWS]
    o_ref[...] = input_ref[0].astype(F32) * convolved


def gate_call(rim, hyena_inputs, hyena_filter, gain):
    width = hyena_filter.shape[1]
    return pl.pallas_call(
        gate_kernel,
        out_shape=(kept((ROWS, width), F32), kept((1, width), F32)),
        scratch_shapes=[pltpu.VMEM((8 + ROWS, width), F32)],
        compiler_params=room(8),
    )(rim, hyena_inputs, hyena_filter, gain.reshape(1, -1))


def rim_of(tails):
    size = lax.axis_size("ctx")
    return lax.ppermute(tails, "ctx", [(i, i + 1) for i in range(size - 1)])


def on_device(queries, keys, values, hyena_inputs, hyena_filter, norm_gain):
    ctx = lax.axis_index("ctx")
    x, z, c = ctx // (2 * Z), (ctx // 2) % Z, ctx % 2
    toward = 2 * c - 1
    own, own_all, turned = prepare_call(keys, values, queries)
    other = lax.ppermute(own_all, "ctx", CORES)
    ring = lambda chunk: lax.ppermute(chunk, "ctx", RING)
    after = lambda chunk, token: lax.optimization_barrier((chunk, token))

    same, near_row, far_row = z * 2 * ROWS, c * ROWS, (1 - c) * ROWS
    blocks = [((z + step * toward) % Z) * 2 * ROWS for step in range(5)]
    where = jnp.stack(
        [x, same + near_row, same + far_row]
        + [block + near_row for block in blocks]
        + [block + far_row for block in blocks]
    ).astype(jnp.int32)

    queries_near = (own_all, other, turned, turned)
    above = lax.ppermute(turned, "ctx", DOWN)
    a0, b0 = own, other[:2]
    a1, b1 = ring(a0), ring(b0)
    acc, stat = attend_call(where, queries_near, [(0, a0)], [(NEAR, (0,), None)])
    a1, stat, above = lax.optimization_barrier((a1, stat, above))
    a2 = ring(a1)
    acc, stat = attend_call(where, queries_near, [(1, a1)], [(NEAR, (0,), (acc, stat))])
    stat, late = after(stat, above)
    b1, stat = after(b1, stat)
    queries_all = (own_all, other, above, lax.ppermute(late, "ctx", CORES))
    b2 = ring(b1)
    high = attend_call(where, queries_all, [(0, a0), (1, a1)], [(ABOVE, (0, 1), None)])
    a2, mark = after(a2, high[1])
    a3 = ring(a2)
    high = attend_call(
        where, queries_all, [(6, b1), (2, a2)], [(ABOVE, (0, 1), (high[0], mark))]
    )
    b2, mark = after(b2, high[1])
    b3 = ring(b2)
    near = attend_call(
        where,
        queries_near,
        [(6, b1), (2, a2), (7, b2)],
        [(NEAR, (0, 1, 2), (acc, stat))],
    )
    stat = near[1]
    a4 = ring(a3)
    *near, acc, stat = attend_call(
        where,
        queries_all,
        [(7, b2), (3, a3), (8, b3)],
        [(NEAR, (1, 2), (near[0], stat)), (ABOVE, (0, 1, 2), (high[0], mark))],
    )
    near, far = attend_call(
        where,
        queries_all,
        [(4, a4)],
        [(NEAR, (0,), near), (ABOVE, (0,), (acc, stat))],
        True,
    )
    crossed = lax.ppermute(far, "ctx", CORES)
    tails = hyena_inputs[1:, ROWS - hyena_filter.shape[0] + 1 :, :]
    tails, below = after(tails, merge_call(near, crossed))
    rim = rim_of(tails)
    gate, gain = gate_call(rim, hyena_inputs, hyena_filter, norm_gain)
    across, gain = after(lax.ppermute(below, "ctx", UP), gain)
    group = lax.axis_size("heads")
    attention, squares = combine_call(
        where, near, crossed, across, group
    )
    spread = lax.all_to_all(squares, "heads", 0, 0, tiled=True)
    wide = turn_call(attention, gain)
    return finish_call(spread, wide, gate)


def solution(mesh):
    placed = (
        P("ctx", "heads"),
        P("ctx", "heads"),
        P("ctx", "heads"),
        P(None, "ctx", "heads"),
        P(None, "heads"),
        P("heads"),
    )
    return jax.shard_map(
        on_device, mesh=mesh, in_specs=placed, out_specs=P("ctx", "heads"), check_vma=False
    )
```

```python
import functools
import math

import jax
import jax.numpy as jnp
from jax import lax
from jax.experimental import pallas as pl
from jax.experimental.pallas import tpu as pltpu
from jax.sharding import PartitionSpec as P

DH = 128
WIDTH = 8192
Z = 8
ROWS = 256
SCALE2 = math.log2(math.e) / math.sqrt(DH)
LOW = -1e29
HIDDEN = -1e30
F32 = jnp.float32
BF16 = jnp.bfloat16


def chip(x, z, c):
    return (x * Z + z % Z) * 2 + c


RING = [
    (chip(x, z, c), chip(x, z + 1 - 2 * c, c)) for x in range(2) for z in range(Z) for c in range(2)
]
CORES = [(chip(x, z, c), chip(x, z, 1 - c)) for x in range(2) for z in range(Z) for c in range(2)]
DOWN = [(chip(1, z, c), chip(0, z, c)) for z in range(Z) for c in range(2)]
CROSS = [(chip(1, z, c), chip(0, z, 1 - c)) for z in range(Z) for c in range(2)]
UP = [(chip(0, z, c), chip(1, z, c)) for z in range(Z) for c in range(2)]


def kept(shape, dtype):
    return pltpu.VMEM(shape, dtype)


def room(mebibytes):
    return pltpu.CompilerParams(vmem_limit_bytes=mebibytes * 1024 * 1024)


def rows_placed(count, numbered):
    row = lax.broadcasted_iota(jnp.int32, (count, ROWS), 0)
    result = jnp.zeros((count, ROWS), F32)
    for number, value in numbered:
        result = jnp.where(row == number, value, result)
    return result


def exact_parts(value):
    high = value.astype(BF16).astype(F32)
    rest = value - high
    middle = rest.astype(BF16).astype(F32)
    return high, middle, rest - middle


def corner(h):
    return slice(h % 2 * DH, (h % 2 + 1) * DH), slice(h // 2 * ROWS, (h // 2 + 1) * ROWS)


def prepare_kernel(heads, k_ref, v_ref, q_ref, pair_ref, triple_ref, turned_ref, held, sems):
    copies = [
        pltpu.make_async_copy(source, target, sems.at[number])
        for number, (source, target) in enumerate(
            (
                (v_ref, held.at[0]),
                (q_ref, held.at[1]),
                (k_ref, pair_ref.at[0]),
                (k_ref, triple_ref.at[0]),
            )
        )
    ]
    for copy in copies:
        copy.start()
    for number, refs in enumerate(
        ((pair_ref.at[1], triple_ref.at[1]), (triple_ref.at[2], turned_ref))
    ):
        copies[number].wait()
        for h in range(heads):
            turned = held[number, :, h * DH : (h + 1) * DH].T
            for ref in refs:
                ref[corner(h)] = turned
    for copy in copies[2:]:
        copy.wait()


def prepare_call(keys, values, queries):
    return pl.pallas_call(
        functools.partial(prepare_kernel, keys.shape[1] // DH),
        out_shape=(
            *(kept((n, *keys.shape), BF16) for n in (2, 3)),
            kept(queries.shape, BF16),
        ),
        in_specs=[pl.BlockSpec(memory_space=pl.ANY)] * 3,
        scratch_shapes=[pltpu.VMEM((2, *values.shape), BF16), pltpu.SemaphoreType.DMA((4,))],
        compiler_params=room(56),
    )(keys, values, queries)


def attend_kernel(places, plan, last, heads, where_ref, *refs):
    query_refs = (refs[0].at[2], refs[1].at[2], refs[2], refs[3])
    held = refs[4 : 4 + len(places)]
    refs = refs[4 + len(places) :]
    carried = 2 * sum(not first for _, _, first in plan)
    given, results = refs[:carried], refs[carried:]
    above = where_ref[0]

    for tiles, used, first in plan:
        chunks, spots = [held[k] for k in used], [places[k] for k in used]
        if not first:
            (acc_in, stat_in), given = given[:2], given[2:]
        if last:
            outs = [results[t % 2].at[t // 2] for t in range(4)]
        else:
            (acc_out, stat_out), results = results[:2], results[2:]

        def run(tiles, masked):
            pieces = [(tile, h) for tile in tiles for h in range(heads)]
            spans = [slice(h * DH, (h + 1) * DH) for h in range(heads)]
            scores = [
                [
                    jnp.dot(
                        chunk[0, :, spans[h]],
                        query_refs[tile][corner(h)],
                        preferred_element_type=F32,
                    )
                    for chunk in chunks
                ]
                for tile, h in pieces
            ]
            if masked:
                drift = lax.broadcasted_iota(jnp.int32, (ROWS, ROWS), 1) - lax.broadcasted_iota(
                    jnp.int32, (ROWS, ROWS), 0
                )
                scores = [
                    [
                        jnp.where(drift >= where_ref[spots[j]] - where_ref[1 + tile], score, HIDDEN)
                        for j, score in enumerate(group)
                    ]
                    for (tile, h), group in zip(pieces, scores)
                ]
            tops = [
                jnp.max(functools.reduce(jnp.maximum, group), axis=0, keepdims=True)
                for group in scores
            ]
            if first:
                tops = [jnp.maximum(top, LOW) for top in tops]
            else:
                old_tops = [stat_in[tile % 2, h : h + 1] for tile, h in pieces]
                tops = [jnp.maximum(top, old) for top, old in zip(tops, old_tops)]
                fades = [jnp.exp2((old - top) * SCALE2) for top, old in zip(tops, old_tops)]
            weights = [
                [jnp.exp2((score - top) * SCALE2) for score in group]
                for group, top in zip(scores, tops)
            ]
            totals = [
                jnp.sum(functools.reduce(jnp.add, group), axis=0, keepdims=True) for group in weights
            ]
            sums = [
                functools.reduce(
                    jnp.add,
                    [
                        jnp.dot(
                            chunk[(1, *corner(h))],
                            weight.astype(BF16),
                            preferred_element_type=F32,
                        )
                        for chunk, weight in zip(chunks, group)
                    ],
                )
                for (tile, h), group in zip(pieces, weights)
            ]
            numbered = {tile: [] for tile in tiles}
            for number, (tile, h) in enumerate(pieces):
                local, span = tile % 2, spans[h]
                top, total, summed = tops[number], totals[number], sums[number]
                if not first:
                    total = total + fades[number] * stat_in[tile % 2, heads + h : heads + h + 1]
                    summed = summed + fades[number] * acc_in[local, span]
                if last:
                    safe = jnp.maximum(total, 1e-30)
                    outs[tile][span] = (summed * (1.0 / safe)).astype(BF16)
                    level = jnp.where(total > 0, top * SCALE2 + jnp.log2(safe), HIDDEN)
                    for k, part in enumerate(exact_parts(level)):
                        numbered[tile].append((k * heads + h, part))
                else:
                    acc_out[local, span] = summed
                    numbered[tile].append((h, top))
                    numbered[tile].append((heads + h, total))
            for tile in tiles:
                if last:
                    outs[tile][heads * DH :] = rows_placed(16, numbered[tile]).astype(BF16)
                else:
                    stat_out[tile % 2] = rows_placed(8, numbered[tile])

        if tiles == NEAR:
            run(tiles, True)
        else:

            @pl.when(above == 0)
            def _():
                run(tiles, False)

            @pl.when(above != 0)
            def _():
                if last:
                    for ref in results:
                        ref[1] = jnp.zeros(ref.shape[1:], BF16)
                else:
                    for ref in (acc_out, stat_out):
                        ref[...] = jnp.zeros(ref.shape, F32)


NEAR, ABOVE = (0, 1), (2, 3)


def attend_call(where, queries, numbered, plan, last=False):
    places, chunks = [3 + number for number, _ in numbered], [chunk for _, chunk in numbered]
    width = queries[2].shape[1]
    heads = width // DH
    operands = [*queries, *chunks, *(array for _, _, state in plan for array in state or ())]
    if last:
        out_shape = tuple(kept((2, width + 16, ROWS), BF16) for _ in range(2))
    else:
        out_shape = tuple(
            kept((2, rows, ROWS), F32) for _ in plan for rows in (width, 8)
        )
    work = 2 * ROWS * ROWS * sum(len(used) for _, used, _ in plan)
    return pl.pallas_call(
        functools.partial(
            attend_kernel,
            places,
            [(tiles, used, state is None) for tiles, used, state in plan],
            last,
            heads,
        ),
        out_shape=out_shape,
        in_specs=[pl.BlockSpec(memory_space=pltpu.SMEM)]
        + [pl.BlockSpec(memory_space=pltpu.VMEM)] * len(operands),
        compiler_params=room(8 + 6 * len(chunks)),
        cost_estimate=pl.CostEstimate(
            flops=4 * work * width,
            bytes_accessed=2 * work * heads,
            transcendentals=work * heads,
        ),
    )(where, *operands)


def levels_of(ref, heads):
    tail = ref[heads * DH :].astype(F32)
    return tail[:heads] + tail[heads : 2 * heads] + tail[2 * heads : 3 * heads]


def shares_of(levels):
    top = functools.reduce(jnp.maximum, levels)
    shares = [jnp.exp2(level - top) for level in levels]
    total = functools.reduce(jnp.add, shares)
    return [share / total for share in shares], top + jnp.log2(total)


def blended(refs, shares, h):
    span = slice(h * DH, (h + 1) * DH)
    return functools.reduce(
        jnp.add, [ref[span].astype(F32) * share[h : h + 1] for ref, share in zip(refs, shares)]
    )


def merge_kernel(heads, a_ref, b_ref, o_ref):
    refs = (a_ref.at[1], b_ref.at[1])
    shares, level = shares_of([levels_of(ref, heads) for ref in refs])
    for h in range(heads):
        o_ref[h * DH : (h + 1) * DH] = blended(refs, shares, h).astype(BF16)
    parts = [
        (k * heads + h, part[h : h + 1])
        for k, part in enumerate(exact_parts(level))
        for h in range(heads)
    ]
    o_ref[heads * DH :] = rows_placed(16, parts).astype(BF16)


def merge_call(a, b):
    heads = a.shape[1] // DH
    return pl.pallas_call(
        functools.partial(merge_kernel, heads),
        out_shape=kept(a.shape[1:], BF16),
        compiler_params=room(8),
    )(a, b)


def combine_kernel(heads, where_ref, a_ref, b_ref, s_ref, att_ref, square_ref):
    refs = (a_ref.at[0], b_ref.at[0], s_ref)
    levels = [levels_of(ref, heads) for ref in refs]
    levels[2] = jnp.where(where_ref[0] != 0, levels[2], HIDDEN)
    shares, _ = shares_of(levels)
    squares = jnp.zeros((DH, ROWS), F32)
    for h in range(heads):
        half = blended(refs, shares, h).astype(BF16)
        att_ref[h * DH : (h + 1) * DH] = half
        wide = half.astype(F32)
        squares = squares + wide * wide
    square_ref[...] = jnp.broadcast_to(
        jnp.sum(squares, axis=0, keepdims=True)[None], square_ref.shape
    )


def combine_call(where, a, b, s, group):
    heads = s.shape[0] // DH
    return pl.pallas_call(
        functools.partial(combine_kernel, heads),
        out_shape=(
            kept((heads * DH, ROWS), BF16),
            kept((group, 1, ROWS), F32),
        ),
        in_specs=[pl.BlockSpec(memory_space=pltpu.SMEM)]
        + [pl.BlockSpec(memory_space=pltpu.VMEM)] * 3,
        compiler_params=room(8),
    )(where, a, b, s)


def turn_kernel(heads, att_ref, gain_ref, o_ref):
    for h in range(heads):
        span = slice(h * DH, (h + 1) * DH)
        o_ref[:, span] = att_ref[span].astype(F32).T * gain_ref[:, span]


def turn_call(attention, gain):
    return pl.pallas_call(
        functools.partial(turn_kernel, attention.shape[0] // DH),
        out_shape=kept(attention.shape[::-1], F32),
        compiler_params=room(8),
    )(attention, gain)


def finish_kernel(heads, spread_ref, wide_ref, hyena_ref, o_ref):
    factor = lax.rsqrt(jnp.sum(spread_ref[...], axis=0) / WIDTH + 1e-06)
    factor = jnp.broadcast_to(factor, (DH, ROWS)).T
    for h in range(heads):
        span = slice(h * DH, (h + 1) * DH)
        o_ref[:, span] = (wide_ref[:, span] * factor + hyena_ref[:, span]).astype(BF16)


def finish_call(spread, wide, hyena_out):
    return pl.pallas_call(
        functools.partial(finish_kernel, wide.shape[1] // DH),
        out_shape=jax.ShapeDtypeStruct(wide.shape, BF16),
        compiler_params=room(8),
    )(spread, wide, hyena_out)


def gate_kernel(rim_ref, input_ref, filter_ref, gain_ref, o_ref, gain_out, product):
    gain_out[...] = gain_ref[...]
    rim_rows = rim_ref.shape[1]
    product[8 - rim_rows : 8] = rim_ref[0].astype(F32) * rim_ref[1].astype(F32)
    product[8:] = input_ref[1].astype(F32) * input_ref[2].astype(F32)
    convolved = filter_ref[0:1] * product[8:]
    for tap in range(1, rim_rows + 1):
        convolved = convolved + filter_ref[tap : tap + 1] * product[8 - tap : 8 - tap + ROWS]
    o_ref[...] = input_ref[0].astype(F32) * convolved


def gate_call(rim, hyena_inputs, hyena_filter, gain):
    width = hyena_filter.shape[1]
    return pl.pallas_call(
        gate_kernel,
        out_shape=(kept((ROWS, width), F32), kept((1, width), F32)),
        scratch_shapes=[pltpu.VMEM((8 + ROWS, width), F32)],
        compiler_params=room(8),
    )(rim, hyena_inputs, hyena_filter, gain.reshape(1, -1))


def rim_of(tails):
    size = lax.axis_size("ctx")
    return lax.ppermute(tails, "ctx", [(i, i + 1) for i in range(size - 1)])


def on_device(queries, keys, values, hyena_inputs, hyena_filter, norm_gain):
    ctx = lax.axis_index("ctx")
    x, z, c = ctx // (2 * Z), (ctx // 2) % Z, ctx % 2
    toward = 2 * c - 1
    own, own_all, turned = prepare_call(keys, values, queries)
    other = lax.ppermute(own_all, "ctx", CORES)
    ring = lambda chunk: lax.ppermute(chunk, "ctx", RING)
    after = lambda chunk, token: lax.optimization_barrier((chunk, token))

    same, near_row, far_row = z * 2 * ROWS, c * ROWS, (1 - c) * ROWS
    blocks = [((z + step * toward) % Z) * 2 * ROWS for step in range(5)]
    where = jnp.stack(
        [x, same + near_row, same + far_row]
        + [block + near_row for block in blocks]
        + [block + far_row for block in blocks]
    ).astype(jnp.int32)

    queries_near = (own_all, other, turned, turned)
    above = lax.ppermute(turned, "ctx", DOWN)
    a0, b0 = own, other[:2]
    a1, b1 = ring(a0), ring(b0)
    acc, stat = attend_call(where, queries_near, [(0, a0)], [(NEAR, (0,), None)])
    a1, stat, above = lax.optimization_barrier((a1, stat, above))
    a2 = ring(a1)
    stat, late = after(stat, above)
    b1, stat = after(b1, stat)
    queries_all = (own_all, other, above, lax.ppermute(late, "ctx", CORES))
    b2 = ring(b1)
    acc, stat, *high = attend_call(
        where,
        queries_all,
        [(0, a0), (1, a1)],
        [(NEAR, (1,), (acc, stat)), (ABOVE, (0, 1), None)],
    )
    a2, mark = after(a2, high[1])
    a3 = ring(a2)
    high = attend_call(
        where, queries_all, [(6, b1), (2, a2)], [(ABOVE, (0, 1), (high[0], mark))]
    )
    b2, mark = after(b2, high[1])
    b3 = ring(b2)
    near = attend_call(
        where,
        queries_near,
        [(6, b1), (2, a2), (7, b2)],
        [(NEAR, (0, 1, 2), (acc, stat))],
    )
    stat = near[1]
    a4 = ring(a3)
    *near, acc, stat = attend_call(
        where,
        queries_all,
        [(7, b2), (3, a3), (8, b3)],
        [(NEAR, (1, 2), (near[0], stat)), (ABOVE, (0, 1, 2), (high[0], mark))],
    )
    near, far = attend_call(
        where,
        queries_all,
        [(4, a4)],
        [(NEAR, (0,), near), (ABOVE, (0,), (acc, stat))],
        True,
    )
    crossed = lax.ppermute(far, "ctx", CORES)
    tails = hyena_inputs[1:, ROWS - hyena_filter.shape[0] + 1 :, :]
    tails, below = after(tails, merge_call(near, crossed))
    rim = rim_of(tails)
    gate, gain = gate_call(rim, hyena_inputs, hyena_filter, norm_gain)
    across, gain = after(lax.ppermute(below, "ctx", UP), gain)
    group = lax.axis_size("heads")
    attention, squares = combine_call(
        where, near, crossed, across, group
    )
    spread = lax.all_to_all(squares, "heads", 0, 0, tiled=True)
    wide = turn_call(attention, gain)
    return finish_call(spread, wide, gate)


def solution(mesh):
    placed = (
        P("ctx", "heads"),
        P("ctx", "heads"),
        P("ctx", "heads"),
        P(None, "ctx", "heads"),
        P(None, "heads"),
        P("heads"),
    )
    return jax.shard_map(
        on_device, mesh=mesh, in_specs=placed, out_specs=P("ctx", "heads"), check_vma=False
    )
```

```python
import functools
import math

import jax
import jax.numpy as jnp
from jax import lax
from jax.experimental import pallas as pl
from jax.experimental.pallas import tpu as pltpu
from jax.sharding import PartitionSpec as P

DH = 128
WIDTH = 8192
Z = 8
ROWS = 256
SCALE2 = math.log2(math.e) / math.sqrt(DH)
LOW = -1e29
HIDDEN = -1e30
F32 = jnp.float32
BF16 = jnp.bfloat16


def chip(x, z, c):
    return (x * Z + z % Z) * 2 + c


RING = [
    (chip(x, z, c), chip(x, z + 1 - 2 * c, c)) for x in range(2) for z in range(Z) for c in range(2)
]
CORES = [(chip(x, z, c), chip(x, z, 1 - c)) for x in range(2) for z in range(Z) for c in range(2)]
DOWN = [(chip(1, z, c), chip(0, z, c)) for z in range(Z) for c in range(2)]
CROSS = [(chip(1, z, c), chip(0, z, 1 - c)) for z in range(Z) for c in range(2)]
UP = [(chip(0, z, c), chip(1, z, c)) for z in range(Z) for c in range(2)]


def kept(shape, dtype):
    return pltpu.VMEM(shape, dtype)


def room(mebibytes):
    return pltpu.CompilerParams(vmem_limit_bytes=mebibytes * 1024 * 1024)


def rows_placed(count, numbered):
    row = lax.broadcasted_iota(jnp.int32, (count, ROWS), 0)
    result = jnp.zeros((count, ROWS), F32)
    for number, value in numbered:
        result = jnp.where(row == number, value, result)
    return result


def exact_parts(value):
    high = value.astype(BF16).astype(F32)
    rest = value - high
    middle = rest.astype(BF16).astype(F32)
    return high, middle, rest - middle


def corner(h):
    return slice(h % 2 * DH, (h % 2 + 1) * DH), slice(h // 2 * ROWS, (h // 2 + 1) * ROWS)


def prepare_kernel(heads, k_ref, v_ref, q_ref, pair_ref, triple_ref, turned_ref, held, sems):
    copies = [
        pltpu.make_async_copy(source, target, sems.at[number])
        for number, (source, target) in enumerate(
            (
                (v_ref, held.at[0]),
                (q_ref, held.at[1]),
                (k_ref, pair_ref.at[0]),
                (k_ref, triple_ref.at[0]),
            )
        )
    ]
    for copy in copies:
        copy.start()
    for number, refs in enumerate(
        ((pair_ref.at[1], triple_ref.at[1]), (triple_ref.at[2], turned_ref))
    ):
        copies[number].wait()
        for h in range(heads):
            turned = held[number, :, h * DH : (h + 1) * DH].T
            for ref in refs:
                ref[corner(h)] = turned
    for copy in copies[2:]:
        copy.wait()


def prepare_call(keys, values, queries):
    return pl.pallas_call(
        functools.partial(prepare_kernel, keys.shape[1] // DH),
        out_shape=(
            *(kept((n, *keys.shape), BF16) for n in (2, 3)),
            kept(queries.shape, BF16),
        ),
        in_specs=[pl.BlockSpec(memory_space=pl.ANY)] * 3,
        scratch_shapes=[pltpu.VMEM((2, *values.shape), BF16), pltpu.SemaphoreType.DMA((4,))],
        compiler_params=room(56),
    )(keys, values, queries)


def attend_kernel(places, plan, last, heads, where_ref, *refs):
    query_refs = (refs[0].at[2], refs[1].at[2], refs[2], refs[3])
    held = refs[4 : 4 + len(places)]
    refs = refs[4 + len(places) :]
    carried = 2 * sum(not first for _, _, first in plan)
    given, results = refs[:carried], refs[carried:]
    above = where_ref[0]

    for tiles, used, first in plan:
        chunks, spots = [held[k] for k in used], [places[k] for k in used]
        if not first:
            (acc_in, stat_in), given = given[:2], given[2:]
        if last:
            outs = [results[t % 2].at[t // 2] for t in range(4)]
        else:
            (acc_out, stat_out), results = results[:2], results[2:]

        def run(tiles, masked):
            pieces = [(tile, h) for tile in tiles for h in range(heads)]
            spans = [slice(h * DH, (h + 1) * DH) for h in range(heads)]
            scores = [
                [
                    jnp.dot(
                        chunk[0, :, spans[h]],
                        query_refs[tile][corner(h)],
                        preferred_element_type=F32,
                    )
                    for chunk in chunks
                ]
                for tile, h in pieces
            ]
            if masked:
                drift = lax.broadcasted_iota(jnp.int32, (ROWS, ROWS), 1) - lax.broadcasted_iota(
                    jnp.int32, (ROWS, ROWS), 0
                )
                scores = [
                    [
                        jnp.where(drift >= where_ref[spots[j]] - where_ref[1 + tile], score, HIDDEN)
                        for j, score in enumerate(group)
                    ]
                    for (tile, h), group in zip(pieces, scores)
                ]
            tops = [
                jnp.max(functools.reduce(jnp.maximum, group), axis=0, keepdims=True)
                for group in scores
            ]
            if first:
                tops = [jnp.maximum(top, LOW) for top in tops]
            else:
                old_tops = [stat_in[tile % 2, h : h + 1] for tile, h in pieces]
                tops = [jnp.maximum(top, old) for top, old in zip(tops, old_tops)]
                fades = [jnp.exp2((old - top) * SCALE2) for top, old in zip(tops, old_tops)]
            weights = [
                [jnp.exp2((score - top) * SCALE2) for score in group]
                for group, top in zip(scores, tops)
            ]
            totals = [
                jnp.sum(functools.reduce(jnp.add, group), axis=0, keepdims=True) for group in weights
            ]
            sums = [
                functools.reduce(
                    jnp.add,
                    [
                        jnp.dot(
                            chunk[(1, *corner(h))],
                            weight.astype(BF16),
                            preferred_element_type=F32,
                        )
                        for chunk, weight in zip(chunks, group)
                    ],
                )
                for (tile, h), group in zip(pieces, weights)
            ]
            numbered = {tile: [] for tile in tiles}
            for number, (tile, h) in enumerate(pieces):
                local, span = tile % 2, spans[h]
                top, total, summed = tops[number], totals[number], sums[number]
                if not first:
                    total = total + fades[number] * stat_in[tile % 2, heads + h : heads + h + 1]
                    summed = summed + fades[number] * acc_in[local, span]
                if last:
                    safe = jnp.maximum(total, 1e-30)
                    outs[tile][span] = (summed * (1.0 / safe)).astype(BF16)
                    level = jnp.where(total > 0, top * SCALE2 + jnp.log2(safe), HIDDEN)
                    for k, part in enumerate(exact_parts(level)):
                        numbered[tile].append((k * heads + h, part))
                else:
                    acc_out[local, span] = summed
                    numbered[tile].append((h, top))
                    numbered[tile].append((heads + h, total))
            for tile in tiles:
                if last:
                    outs[tile][heads * DH :] = rows_placed(16, numbered[tile]).astype(BF16)
                else:
                    stat_out[tile % 2] = rows_placed(8, numbered[tile])

        if tiles == NEAR:
            run(tiles, True)
        else:

            @pl.when(above == 0)
            def _():
                run(tiles, False)

            @pl.when(above != 0)
            def _():
                if last:
                    for ref in results:
                        ref[1] = jnp.zeros(ref.shape[1:], BF16)
                else:
                    for ref in (acc_out, stat_out):
                        ref[...] = jnp.zeros(ref.shape, F32)


NEAR, ABOVE = (0, 1), (2, 3)


def attend_call(where, queries, numbered, plan, last=False):
    places, chunks = [3 + number for number, _ in numbered], [chunk for _, chunk in numbered]
    width = queries[2].shape[1]
    heads = width // DH
    operands = [*queries, *chunks, *(array for _, _, state in plan for array in state or ())]
    if last:
        out_shape = tuple(kept((2, width + 16, ROWS), BF16) for _ in range(2))
    else:
        out_shape = tuple(
            kept((2, rows, ROWS), F32) for _ in plan for rows in (width, 8)
        )
    work = 2 * ROWS * ROWS * sum(len(used) for _, used, _ in plan)
    return pl.pallas_call(
        functools.partial(
            attend_kernel,
            places,
            [(tiles, used, state is None) for tiles, used, state in plan],
            last,
            heads,
        ),
        out_shape=out_shape,
        in_specs=[pl.BlockSpec(memory_space=pltpu.SMEM)]
        + [pl.BlockSpec(memory_space=pltpu.VMEM)] * len(operands),
        compiler_params=room(8 + 6 * len(chunks)),
        cost_estimate=pl.CostEstimate(
            flops=4 * work * width,
            bytes_accessed=2 * work * heads,
            transcendentals=work * heads,
        ),
    )(where, *operands)


def levels_of(ref, heads):
    tail = ref[heads * DH :].astype(F32)
    return tail[:heads] + tail[heads : 2 * heads] + tail[2 * heads : 3 * heads]


def shares_of(levels):
    top = functools.reduce(jnp.maximum, levels)
    shares = [jnp.exp2(level - top) for level in levels]
    total = functools.reduce(jnp.add, shares)
    return [share / total for share in shares], top + jnp.log2(total)


def blended(refs, shares, h):
    span = slice(h * DH, (h + 1) * DH)
    return functools.reduce(
        jnp.add, [ref[span].astype(F32) * share[h : h + 1] for ref, share in zip(refs, shares)]
    )


def merge_kernel(heads, a_ref, b_ref, o_ref):
    refs = (a_ref.at[1], b_ref.at[1])
    shares, level = shares_of([levels_of(ref, heads) for ref in refs])
    for h in range(heads):
        o_ref[h * DH : (h + 1) * DH] = blended(refs, shares, h).astype(BF16)
    parts = [
        (k * heads + h, part[h : h + 1])
        for k, part in enumerate(exact_parts(level))
        for h in range(heads)
    ]
    o_ref[heads * DH :] = rows_placed(16, parts).astype(BF16)


def merge_call(a, b):
    heads = a.shape[1] // DH
    return pl.pallas_call(
        functools.partial(merge_kernel, heads),
        out_shape=kept(a.shape[1:], BF16),
        compiler_params=room(8),
    )(a, b)


def combine_kernel(heads, where_ref, a_ref, b_ref, s_ref, att_ref, square_ref):
    refs = (a_ref.at[0], b_ref.at[0], s_ref)
    levels = [levels_of(ref, heads) for ref in refs]
    levels[2] = jnp.where(where_ref[0] != 0, levels[2], HIDDEN)
    shares, _ = shares_of(levels)
    squares = jnp.zeros((DH, ROWS), F32)
    for h in range(heads):
        half = blended(refs, shares, h).astype(BF16)
        att_ref[h * DH : (h + 1) * DH] = half
        wide = half.astype(F32)
        squares = squares + wide * wide
    square_ref[...] = jnp.broadcast_to(
        jnp.sum(squares, axis=0, keepdims=True)[None], square_ref.shape
    )


def combine_call(where, a, b, s, group):
    heads = s.shape[0] // DH
    return pl.pallas_call(
        functools.partial(combine_kernel, heads),
        out_shape=(
            kept((heads * DH, ROWS), BF16),
            kept((group, 1, ROWS), F32),
        ),
        in_specs=[pl.BlockSpec(memory_space=pltpu.SMEM)]
        + [pl.BlockSpec(memory_space=pltpu.VMEM)] * 3,
        compiler_params=room(8),
    )(where, a, b, s)


def turn_kernel(heads, att_ref, gain_ref, o_ref):
    for h in range(heads):
        span = slice(h * DH, (h + 1) * DH)
        o_ref[:, span] = att_ref[span].astype(F32).T * gain_ref[:, span]


def turn_call(attention, gain):
    return pl.pallas_call(
        functools.partial(turn_kernel, attention.shape[0] // DH),
        out_shape=kept(attention.shape[::-1], F32),
        compiler_params=room(8),
    )(attention, gain)


def finish_kernel(heads, spread_ref, wide_ref, hyena_ref, o_ref):
    factor = lax.rsqrt(jnp.sum(spread_ref[...], axis=0) / WIDTH + 1e-06)
    factor = jnp.broadcast_to(factor, (DH, ROWS)).T
    for h in range(heads):
        span = slice(h * DH, (h + 1) * DH)
        o_ref[:, span] = (wide_ref[:, span] * factor + hyena_ref[:, span]).astype(BF16)


def finish_call(spread, wide, hyena_out):
    return pl.pallas_call(
        functools.partial(finish_kernel, wide.shape[1] // DH),
        out_shape=jax.ShapeDtypeStruct(wide.shape, BF16),
        compiler_params=room(8),
    )(spread, wide, hyena_out)


def gate_kernel(rim_ref, input_ref, filter_ref, gain_ref, o_ref, gain_out, product):
    gain_out[...] = gain_ref[...]
    rim_rows = rim_ref.shape[1]
    product[8 - rim_rows : 8] = rim_ref[0].astype(F32) * rim_ref[1].astype(F32)
    product[8:] = input_ref[1].astype(F32) * input_ref[2].astype(F32)
    convolved = filter_ref[0:1] * product[8:]
    for tap in range(1, rim_rows + 1):
        convolved = convolved + filter_ref[tap : tap + 1] * product[8 - tap : 8 - tap + ROWS]
    o_ref[...] = input_ref[0].astype(F32) * convolved


def gate_call(rim, hyena_inputs, hyena_filter, gain):
    width = hyena_filter.shape[1]
    return pl.pallas_call(
        gate_kernel,
        out_shape=(kept((ROWS, width), F32), kept((1, width), F32)),
        scratch_shapes=[pltpu.VMEM((8 + ROWS, width), F32)],
        compiler_params=room(8),
    )(rim, hyena_inputs, hyena_filter, gain.reshape(1, -1))


def rim_of(tails):
    size = lax.axis_size("ctx")
    return lax.ppermute(tails, "ctx", [(i, i + 1) for i in range(size - 1)])


def on_device(queries, keys, values, hyena_inputs, hyena_filter, norm_gain):
    ctx = lax.axis_index("ctx")
    x, z, c = ctx // (2 * Z), (ctx // 2) % Z, ctx % 2
    toward = 2 * c - 1
    own, own_all, turned = prepare_call(keys, values, queries)
    other = lax.ppermute(own_all, "ctx", CORES)
    ring = lambda chunk: lax.ppermute(chunk, "ctx", RING)
    after = lambda chunk, token: lax.optimization_barrier((chunk, token))

    same, near_row, far_row = z * 2 * ROWS, c * ROWS, (1 - c) * ROWS
    blocks = [((z + step * toward) % Z) * 2 * ROWS for step in range(5)]
    where = jnp.stack(
        [x, same + near_row, same + far_row]
        + [block + near_row for block in blocks]
        + [block + far_row for block in blocks]
    ).astype(jnp.int32)

    queries_near = (own_all, other, turned, turned)
    above = lax.ppermute(turned, "ctx", DOWN)
    a0, b0 = own, other[:2]
    a1, b1 = ring(a0), ring(b0)
    acc, stat = attend_call(where, queries_near, [(0, a0)], [(NEAR, (0,), None)])
    a1, stat, above = lax.optimization_barrier((a1, stat, above))
    a2 = ring(a1)
    stat, late = after(stat, above)
    b1, stat = after(b1, stat)
    queries_all = (own_all, other, above, lax.ppermute(late, "ctx", CORES))
    b2 = ring(b1)
    acc, stat, *high = attend_call(
        where,
        queries_all,
        [(0, a0), (1, a1)],
        [(NEAR, (1,), (acc, stat)), (ABOVE, (0, 1), None)],
    )
    a2, mark = after(a2, high[1])
    a3 = ring(a2)
    acc, stat, *high = attend_call(
        where,
        queries_all,
        [(6, b1), (2, a2)],
        [(NEAR, (0, 1), (acc, stat)), (ABOVE, (0, 1), (high[0], mark))],
    )
    b2, mark = after(b2, high[1])
    b3 = ring(b2)
    a4 = ring(a3)
    *near, acc, stat = attend_call(
        where,
        queries_all,
        [(7, b2), (3, a3), (8, b3)],
        [(NEAR, (0, 1, 2), (acc, stat)), (ABOVE, (0, 1, 2), (high[0], mark))],
    )
    near, far = attend_call(
        where,
        queries_all,
        [(4, a4)],
        [(NEAR, (0,), near), (ABOVE, (0,), (acc, stat))],
        True,
    )
    crossed = lax.ppermute(far, "ctx", CORES)
    tails = hyena_inputs[1:, ROWS - hyena_filter.shape[0] + 1 :, :]
    tails, below = after(tails, merge_call(near, crossed))
    rim = rim_of(tails)
    gate, gain = gate_call(rim, hyena_inputs, hyena_filter, norm_gain)
    across, gain = after(lax.ppermute(below, "ctx", UP), gain)
    group = lax.axis_size("heads")
    attention, squares = combine_call(
        where, near, crossed, across, group
    )
    spread = lax.all_to_all(squares, "heads", 0, 0, tiled=True)
    wide = turn_call(attention, gain)
    return finish_call(spread, wide, gate)


def solution(mesh):
    placed = (
        P("ctx", "heads"),
        P("ctx", "heads"),
        P("ctx", "heads"),
        P(None, "ctx", "heads"),
        P(None, "heads"),
        P("heads"),
    )
    return jax.shard_map(
        on_device, mesh=mesh, in_specs=placed, out_specs=P("ctx", "heads"), check_vma=False
    )
```
